128 devices in a mesh: slab: 8 (over z_lo, x), band: 16 (over z_hi, y, core).
Axes of the slice: x: 4, y: 4, z: 4 (z_hi: 2, z_lo: 2; z = z_hi * 2 + z_lo), core: 2. Of those that a mesh axis runs over, the one named last changes fastest.
Arguments:
- orbitals: float32 [384, 96, 2304], P('band', 'slab'), may hold values from -20 to 20
- potential: float32 [96, 2304], P('slab'), may hold values from -3 to 1
Outputs:
- filtered: float32 [384, 96, 2304], P('band', 'slab')
- correlation: float32 [384, 384], P('band', 'slab')
- projected: float32 [384, 384], P('band', 'slab')
The draws below stay inside these ranges and needn't reach their ends.
All inputs are finite; a program needn't handle non-finite values.
Results may differ from the reference program's by a relative error of at most 0.00016.
Values sent between devices are 32-bit elements; how exact they have to be, the bound alone decides.
A program may use at most 128 MiB of HBM per device.

```python
import math
import jax
import jax.numpy as jnp
from jax import lax

ORB_DEV = 24
NX = 48
NY = 48
NXY = 2304
NZ = 96
ORBITALS = 384


def draw_orbitals(key, part):
    key = jax.random.fold_in(key, 7)
    key_noise, key_coef, key_wave, key_phase = jax.random.split(key, 4)
    index = jnp.arange(NZ * NXY, dtype=jnp.int32)
    coord_z = (index // NXY).astype(jnp.float32)
    coord_y = (index % NXY // NX).astype(jnp.float32)
    coord_x = (index % NX).astype(jnp.float32)
    waves = jax.random.randint(key_wave, (8, 3), -2, 3).astype(jnp.float32)
    phases = jax.random.uniform(key_phase, (8,), jnp.float32, -math.pi, math.pi)
    noise = jnp.clip(jax.random.normal(key_noise, (ORBITALS, NZ, NXY), jnp.float32), -4.0, 4.0)
    coef_scale = 0.5
    coef = jnp.clip(jax.random.normal(key_coef, (ORBITALS, 8), jnp.float32) * coef_scale, -2.0, 2.0)
    grid_field = noise
    for number in range(8):
        angle = 2.0 * math.pi * (waves[number, 0] * coord_x / NX + waves[number, 1] * coord_y / NY + waves[number, 2] * coord_z / NZ) + phases[number]
        wave_field = jnp.cos(angle).reshape(NZ, NXY)
        grid_field = grid_field + coef[:, number, None, None] * wave_field[None]
    return grid_field.astype(jnp.float32)


def levels(own_key, extent, cuts, least, top_value):
    factor_of = 1.0
    for axis_at, shards_of in cuts:
        heights = jax.random.uniform(jax.random.fold_in(jax.random.fold_in(own_key, 6), axis_at), (shards_of,), jnp.float32, least / len(cuts), top_value / len(cuts))
        factor_of = factor_of * jnp.repeat(jnp.exp(heights), extent[axis_at] // shards_of).reshape((-1,) + (1,) * (len(extent) - 1 - axis_at))
    return factor_of


def setup_inputs(seed: int = 0) -> dict:
    streams_of = jax.random.split(jax.random.key(seed), 3)
    return {
        "orbitals": draw_orbitals(jax.random.fold_in(streams_of[2], 71), 0),
        "potential": jnp.clip(-3.0 + 4.0 * jax.random.uniform(streams_of[1], (NZ, NXY), jnp.float32) ** levels(streams_of[1], (NZ, NXY), ((0, 8),), -0.2, 0.2), -3.0, 1.0),
    }


SPACING = 0.32
STENCIL = 1.0 / (12.0 * SPACING * SPACING)
CENTER = 38.0
HALF_WIDTH = 42.0


def hamiltonian(orbital_block, potential):
    rows = orbital_block.shape[0]
    lattice = orbital_block.reshape(rows, NZ, NY, NX)
    laplace = -90.0 * lattice
    for dimension in (1, 2, 3):
        for offset, weight in ((1, 16.0), (2, -1.0)):
            laplace = laplace + weight * (jnp.roll(lattice, offset, dimension) + jnp.roll(lattice, -offset, dimension))
    laplace = laplace.reshape(orbital_block.shape)
    return -0.5 * STENCIL * laplace + potential[None] * orbital_block


def filter_block(orbital_block, potential):
    section_one = (hamiltonian(orbital_block, potential) - CENTER * orbital_block) / HALF_WIDTH
    filtered = 2.0 * (hamiltonian(section_one, potential) - CENTER * section_one) / HALF_WIDTH - orbital_block
    return filtered, hamiltonian(filtered, potential)


def reference(orbitals, potential):
    blocks = orbitals.reshape(ORBITALS // ORB_DEV, ORB_DEV, NZ, NXY)
    filtered, applied = lax.map(lambda blk: filter_block(blk, potential), blocks)
    flat_filtered = filtered.reshape(ORBITALS, NZ * NXY)
    flat_applied = applied.reshape(ORBITALS, NZ * NXY)
    factor = 1.0 / (NZ * NXY)
    contract_dims = (((1,), (1,)), ((), ()))
    correlation = lax.dot_general(flat_filtered, flat_filtered, contract_dims, precision=lax.Precision.HIGHEST, preferred_element_type=jnp.float32) * factor
    projected = lax.dot_general(flat_applied, flat_filtered, contract_dims, precision=lax.Precision.HIGHEST, preferred_element_type=jnp.float32) * factor
    return flat_filtered.reshape(ORBITALS, NZ, NXY), correlation, projected
```

```python
import jax
import jax.numpy as jnp
from jax import lax
from jax.experimental import pallas as pl
from jax.experimental.pallas import tpu as pltpu
from jax.sharding import PartitionSpec as P

NX = 48
NXY = 2304
ORB = 24
PLANES = 12
CHIPS = 8
SLABS = 8
HALF = NXY // 2
CHUNK = 384
CELLS = 221184

SPACING = 0.32
STENCIL = 1.0 / (12.0 * SPACING * SPACING)
CENTER = 38.0
HALF_WIDTH = 42.0
NEAR = -8.0 * STENCIL / HALF_WIDTH
FAR = 0.5 * STENCIL / HALF_WIDTH
MESH = pl.DeviceIdType.MESH

PEERS = ((1, 0), (0, 1), (1, 2), (0, 3), (1, 1), (0, 2), (1, 3))


def dot_nt(a, b):
    return lax.dot_general(a, b, (((1,), (1,)), ((), ())), preferred_element_type=jnp.float32)


def halves(a):
    high = a.astype(jnp.bfloat16)
    return high, (a - high.astype(jnp.float32)).astype(jnp.bfloat16)


def kernel(
    orb_hbm, pot_ref, filt_hbm, corr_ref, proj_ref,
    O, V_in, W, S, F, A, RF, RA, G, R1, B2, R2,
    load_sem, out_sem, halo_s, halo_r, pot_s, pot_r, swap_s, swap_r, own_sem, fwd_s, fwd_r,
    r1_s, r1_r, r2_s, r2_r,
):
    band, slab = lax.axis_index("band"), lax.axis_index("slab")
    chip, core = band // 2, band % 2
    z_hi, y = chip // 4, chip % 4

    def chip_at(offset):
        return ((z_hi + offset[0]) % 2) * 4 + (y + offset[1]) % 4

    def to_band(b):
        return {"band": b, "slab": slab}

    def to_slab(s):
        return {"band": band, "slab": s}

    load = pltpu.make_async_copy(orb_hbm, O.at[pl.ds(6, PLANES)], load_sem)
    load.start()

    up, down = (slab + 1) % SLABS, (slab + SLABS - 1) % SLABS
    partners = [to_band(chip_at(o) * 2 + core) for o in PEERS]
    partners.append(to_band(chip * 2 + 1 - core))
    partners += [to_slab((slab + d) % SLABS) for d in range(1, SLABS)]
    barrier = pltpu.get_barrier_semaphore()
    for partner in partners:
        pl.semaphore_signal(barrier, inc=1, device_id=partner, device_id_type=MESH)
    pl.semaphore_wait(barrier, len(partners))

    sends = []

    def send(src, dst, s_sem, r_sem, where):
        copy = pltpu.make_async_remote_copy(
            src_ref=src, dst_ref=dst, send_sem=s_sem, recv_sem=r_sem,
            device_id=where, device_id_type=MESH,
        )
        copy.start()
        sends.append(copy)
        return copy

    pots = [
        send(pot_ref.at[pl.ds(4, 8)], V_in.at[0], pot_s.at[0], pot_r.at[0], to_slab(up)),
        send(pot_ref.at[pl.ds(0, 8)], V_in.at[1], pot_s.at[1], pot_r.at[1], to_slab(down)),
    ]
    load.wait()
    halos = []
    for t in range(3):
        halos.append((
            send(O.at[pl.ds(16 - 2 * t, 2)], O.at[pl.ds(4 - 2 * t, 2)],
                 halo_s.at[0, t], halo_r.at[0, t], to_slab(up)),
            send(O.at[pl.ds(6 + 2 * t, 2)], O.at[pl.ds(18 + 2 * t, 2)],
                 halo_s.at[1, t], halo_r.at[1, t], to_slab(down)),
        ))

    def fill(z, row):
        weight = (row + (45.0 * STENCIL - CENTER)) * (1.0 / HALF_WIDTH)
        W[z + 4] = jnp.broadcast_to(weight, (8, NXY))

    for z in range(PLANES):
        fill(z, pot_ref[z : z + 1, :])

    x_at = (lax.broadcasted_iota(jnp.int32, (8, CHUNK + 256), 1) + 16) % NX

    def stage(src, src_off, first, count, second, emit):
        total = count if second is None else 2 * count

        def body(i, carry):
            p = i // 3
            z = first + p
            if second is not None:
                z = z + (p // count) * (second - first - count)
            rows = pl.ds(pl.multiple_of((i % 3) * 8, 8), 8)
            at = z + src_off
            for g in range(NXY // CHUNK):
                lanes = pl.ds(g * CHUNK, CHUNK)
                lo, hi = (g * CHUNK - 128) % NXY, (g * CHUNK + CHUNK) % NXY
                v = src[at, rows, lanes]
                wide = jnp.concatenate(
                    [src[at, rows, pl.ds(lo, 128)], v, src[at, rows, pl.ds(hi, 128)]], axis=1
                )
                size = CHUNK + 256

                def cut(a, shift):
                    return pltpu.roll(a, shift % size, 1)[:, 128 : 128 + CHUNK]

                before, after = pltpu.roll(wide, NX, 1), pltpu.roll(wide, size - NX, 1)
                near = before[:, 128 : 128 + CHUNK] + after[:, 128 : 128 + CHUNK]
                near = near + cut(jnp.where(x_at == 0, before, wide), -1)
                near = near + cut(jnp.where(x_at == NX - 1, after, wide), 1)
                near = near + (src[at - 1, rows, lanes] + src[at + 1, rows, lanes])
                far = cut(wide, 2 * NX) + cut(wide, -2 * NX)
                far = far + cut(jnp.where(x_at < 2, before, wide), -2)
                far = far + cut(jnp.where(x_at >= NX - 2, after, wide), 2)
                far = far + (src[at - 2, rows, lanes] + src[at + 2, rows, lanes])
                h = NEAR * near + FAR * far + W[z + 4, :, lanes] * v
                emit(z, rows, lanes, h, v)
            return carry

        lax.fori_loop(0, 3 * total, body, 0)

    def emit_s(z, rows, lanes, h, v):
        S[z + 4, rows, lanes] = h

    def emit_f(z, rows, lanes, h, v):
        F[z + 2, rows, lanes] = 2.0 * h - O[z + 6, rows, lanes]

    def emit_a(z, rows, lanes, h, v):
        A[z, rows, lanes] = HALF_WIDTH * h + CENTER * v

    def stage_s(first, count, second=None):
        stage(O, 6, first, count, second, emit_s)

    def stage_f(first, count, second=None):
        stage(S, 4, first, count, second, emit_f)

    def stage_a(first, count, second=None):
        stage(F, 2, first, count, second, emit_a)

    def swap(kind, q):
        src, off = ((F, 2), (A, 0))[kind]

        def part(c):
            lanes = pl.ds(pl.multiple_of((c % 2) * HALF, 128), HALF)
            return src.at[4 * q + c // 2 + off, :, lanes]

        dst = RF.at[q, chip, core] if kind == 0 else RA.at[q, chip]
        copies = []
        for d, o in enumerate(PEERS):
            c = chip_at(o)
            copies.append(
                send(part(c), dst, swap_s.at[kind, q, d], swap_r.at[kind, q, d], to_band(c * 2 + core))
            )
        own = pltpu.make_async_copy(part(chip), dst, own_sem.at[kind, q])
        own.start()
        return copies, own

    def swap_wait(copies, own):
        own.wait()
        for copy in copies:
            copy.wait_recv()

    def forward(q):
        piece = RF.at[q, :, core]
        return send(piece, piece, fwd_s.at[q], fwd_r.at[q], to_band(chip * 2 + 1 - core))

    def gram(kind, q, start):
        def body(k, carry):
            lanes = pl.ds(pl.multiple_of(k * CHUNK, 128), CHUNK)
            f_high, f_low = halves(RF[q, :, :, :, lanes].reshape(2 * CHIPS * ORB, CHUNK))
            rows = RF[q, :, core, :, lanes] if kind == 0 else RA[q, :, :, lanes]
            high, low = halves(rows.reshape(CHIPS * ORB, CHUNK))
            part = dot_nt(high, f_high) + (dot_nt(high, f_low) + dot_nt(low, f_high))
            G[kind] = G[kind] + part.reshape(CHIPS, ORB, 2 * CHIPS * ORB)
            return carry

        if start:
            G[kind] = jnp.zeros((CHIPS, ORB, 2 * CHIPS * ORB), jnp.float32)
        lax.fori_loop(0, HALF // CHUNK, body, 0)

    def reduce_band(kind):
        copies = []
        for d, o in enumerate(PEERS):
            c = chip_at(o)
            copies.append(
                send(G.at[kind, c], R1.at[kind, d], r1_s.at[kind, d], r1_r.at[kind, d],
                     to_band(c * 2 + core))
            )
        return copies

    def reduce_slab(kind, arrived):
        for copy in arrived:
            copy.wait_recv()
        rows = G[kind, chip]
        for d in range(len(PEERS)):
            rows = rows + R1[kind, d]
        for s in range(SLABS):
            B2[kind, s] = pltpu.roll(rows, (-NX * s) % (NX * SLABS), 1)[:, :128]
        copies = []
        for d in range(1, SLABS):
            s = (slab + d) % SLABS
            copies.append(
                send(B2.at[kind, s], R2.at[kind, d - 1], r2_s.at[kind, d - 1], r2_r.at[kind, d - 1],
                     to_slab(s))
            )
        return copies

    def finish(kind, arrived, out):
        for copy in arrived:
            copy.wait_recv()
        block = B2[kind, slab]
        for d in range(SLABS - 1):
            block = block + R2[kind, d]
        out[...] = block[:, :NX] * (1.0 / CELLS)

    stage_s(2, 8)
    stage_f(4, 4)
    f1 = swap(0, 1)

    for copy in halos[0]:
        copy.wait_recv()
    stage_s(0, 2, 10)
    stage_f(2, 2, 8)
    stage_a(4, 4)
    a1 = swap(1, 1)

    for copy in pots:
        copy.wait_recv()
    for n in range(4):
        fill(n - 4, V_in[0, 4 + n : 5 + n, :])
        fill(12 + n, V_in[1, n : n + 1, :])
    for copy in halos[1]:
        copy.wait_recv()
    stage_s(-2, 2, 12)
    stage_f(0, 2, 10)
    f0, f2 = swap(0, 0), swap(0, 2)
    store = pltpu.make_async_copy(F.at[pl.ds(2, PLANES)], filt_hbm, out_sem)
    store.start()

    swap_wait(*f1)
    w1 = forward(1)
    for copy in halos[2]:
        copy.wait_recv()
    stage_s(-4, 2, 14)
    stage_f(-2, 2, 12)
    stage_a(0, 4, 8)
    a0, a2 = swap(1, 0), swap(1, 2)

    w1.wait_recv()
    gram(0, 1, True)
    swap_wait(*a1)
    gram(1, 1, True)
    swap_wait(*f0)
    w0 = forward(0)
    swap_wait(*f2)
    w2 = forward(2)
    w0.wait_recv()
    gram(0, 0, False)
    w2.wait_recv()
    gram(0, 2, False)
    c1 = reduce_band(0)
    swap_wait(*a0)
    gram(1, 0, False)
    c2 = reduce_slab(0, c1)
    swap_wait(*a2)
    gram(1, 2, False)
    p1 = reduce_band(1)
    finish(0, c2, corr_ref)
    p2 = reduce_slab(1, p1)
    finish(1, p2, proj_ref)
    for copy in sends:
        copy.wait_send()
    store.wait()


def local(orbitals, potential):
    f32 = jnp.float32
    dma = pltpu.SemaphoreType.DMA
    peers = len(PEERS)
    filtered, correlation, projected = pl.pallas_call(
        kernel,
        out_shape=(
            jax.ShapeDtypeStruct((PLANES, ORB, NXY), f32),
            jax.ShapeDtypeStruct((ORB, NX), f32),
            jax.ShapeDtypeStruct((ORB, NX), f32),
        ),
        in_specs=[pl.BlockSpec(memory_space=pl.ANY), pl.BlockSpec(memory_space=pltpu.VMEM)],
        out_specs=(
            pl.BlockSpec(memory_space=pl.ANY),
            pl.BlockSpec(memory_space=pltpu.VMEM),
            pl.BlockSpec(memory_space=pltpu.VMEM),
        ),
        scratch_shapes=[
            pltpu.VMEM((PLANES + 12, ORB, NXY), f32),
            pltpu.VMEM((2, 8, NXY), f32),
            pltpu.VMEM((PLANES + 8, 8, NXY), f32),
            pltpu.VMEM((PLANES + 8, ORB, NXY), f32),
            pltpu.VMEM((PLANES + 4, ORB, NXY), f32),
            pltpu.VMEM((PLANES, ORB, NXY), f32),
            pltpu.VMEM((3, CHIPS, 2, ORB, HALF), f32),
            pltpu.VMEM((3, CHIPS, ORB, HALF), f32),
            pltpu.VMEM((2, CHIPS, ORB, 2 * CHIPS * ORB), f32),
            pltpu.VMEM((2, peers, ORB, 2 * CHIPS * ORB), f32),
            pltpu.VMEM((2, SLABS, ORB, 128), f32),
            pltpu.VMEM((2, SLABS - 1, ORB, 128), f32),
            dma, dma,
            dma((2, 3)), dma((2, 3)),
            dma((2,)), dma((2,)),
            dma((2, 3, peers)), dma((2, 3, peers)),
            dma((2, 3)),
            dma((3,)), dma((3,)),
            dma((2, peers)), dma((2, peers)),
            dma((2, SLABS - 1)), dma((2, SLABS - 1)),
        ],
        compiler_params=pltpu.CompilerParams(
            collective_id=0, has_side_effects=True, vmem_limit_bytes=56 << 20
        ),
        cost_estimate=pl.CostEstimate(
            flops=3_500_000_000, bytes_accessed=6_000_000, transcendentals=0
        ),
    )(jnp.transpose(orbitals, (1, 0, 2)), potential)
    return jnp.transpose(filtered, (1, 0, 2)), correlation, projected


def solution(mesh):
    return jax.shard_map(
        local,
        mesh=mesh,
        in_specs=(P("band", "slab", None), P("slab", None)),
        out_specs=(P("band", "slab", None), P("band", "slab"), P("band", "slab")),
        check_vma=False,
    )
```

```python
import jax
import jax.numpy as jnp
import ml_dtypes
import numpy as np
from jax import lax
from jax.experimental import pallas as pl
from jax.experimental.pallas import tpu as pltpu
from jax.sharding import PartitionSpec as P

NX = 48
NXY = 2304
ORB = 24
PLANES = 12
SLABS = 8
HALF = NXY // 2
CHUNK = 384
CELLS = 221184

SPACING = 0.32
STENCIL = 1.0 / (12.0 * SPACING * SPACING)
CENTER = 38.0
HALF_WIDTH = 42.0
NEAR = -0.5 * STENCIL / HALF_WIDTH
MESH = pl.DeviceIdType.MESH

CHUNK_BASE = (4, 2, 0)
CHUNK_STRIDE = (0, 4, 8)
PEERS = (1, 3, 2)
HALF_ORB = 192
ROWS = 96


def plane_table():
    table = np.zeros((3, 512, 256), np.float32)
    for r in range(3):
        for n in range(256):
            cell = 256 * r + n
            row, x = cell // NX, cell % NX
            for offset, weight in ((1, 16.0), (2, -1.0), (-1, 16.0), (-2, -1.0)):
                table[r, row * NX + (x + offset) % NX - 256 * r + 128, n] += weight
                table[r, n + 128 + offset * NX, n] += weight
    return table.astype(ml_dtypes.bfloat16)


def dot_nt(a, b):
    return lax.dot_general(a, b, (((1,), (1,)), ((), ())), preferred_element_type=jnp.float32)


def halves(a):
    high = a.astype(jnp.bfloat16)
    return high, (a - high.astype(jnp.float32)).astype(jnp.bfloat16)


def kernel(
    orb_hbm, pot_ref, table_hbm, filt_hbm, corr_ref, proj_ref,
    O, T, V_in, W, S, F, A, RF, RA, RA_far, G, G_far, R1, XB, XR, B2, R2,
    load_sem, table_sem, out_sem, halo_s, halo_r, pot_s, pot_r, swap_s, swap_r, own_sem, fwd_s, fwd_r,
    far_s, far_r, early_s, early_r, r1_s, r1_r, x_s, x_r, r2_s, r2_r,
):
    band, slab = lax.axis_index("band"), lax.axis_index("slab")
    chip, core = band // 2, band % 2
    z_hi, y = chip // 4, chip % 4

    def to_band(z, row, side):
        return {"band": z * 8 + row * 2 + side, "slab": slab}

    def to_slab(s):
        return {"band": band, "slab": s}

    load = pltpu.make_async_copy(orb_hbm, O.at[pl.ds(6, PLANES)], load_sem)
    load.start()
    table_load = pltpu.make_async_copy(table_hbm, T, table_sem)
    table_load.start()

    up, down = (slab + 1) % SLABS, (slab + SLABS - 1) % SLABS
    partners = [to_band(z_hi, (y + d) % 4, core) for d in PEERS]
    partners.append(to_band(z_hi, y, 1 - core))
    partners += [to_band(1 - z_hi, row, side) for row in range(4) for side in range(2)]
    partners += [to_slab((slab + d) % SLABS) for d in range(1, SLABS)]
    barrier = pltpu.get_barrier_semaphore()
    for partner in partners:
        pl.semaphore_signal(barrier, inc=1, device_id=partner, device_id_type=MESH)

    sends = []

    def send(src, dst, s_sem, r_sem, where):
        copy = pltpu.make_async_remote_copy(
            src_ref=src, dst_ref=dst, send_sem=s_sem, recv_sem=r_sem,
            device_id=where, device_id_type=MESH,
        )
        copy.start()
        sends.append(copy)
        return copy

    def fill(z, row):
        weight = (row + (45.0 * STENCIL - CENTER)) * (1.0 / HALF_WIDTH)
        W[z + 4] = jnp.broadcast_to(weight, (8, NXY))

    for z in range(PLANES):
        fill(z, pot_ref[z : z + 1, :])

    table_load.wait()
    load.wait()

    def stage(src, src_off, starts, emit):
        count = 4 // len(starts)

        def planes(ref, off, rows, lanes):
            parts = [ref[pl.ds(z + off, count), rows, lanes] for z in starts]
            return parts[0] if len(parts) == 1 else jnp.concatenate(parts, axis=0)

        everything = slice(None)

        def body(i, carry):
            for r in range(3):
                base = i * 768 + 256 * r
                lanes = pl.ds(pl.multiple_of(base, 128), 256)
                left = pl.ds(pl.multiple_of((base + NXY - 128) % NXY, 128), 128)
                right = pl.ds(pl.multiple_of((base + 256) % NXY, 128), 128)
                v = planes(src, src_off, everything, lanes)
                wide = jnp.concatenate(
                    [planes(src, src_off, everything, left), v, planes(src, src_off, everything, right)],
                    axis=2,
                ).reshape(4 * ORB, 512)
                flat = jnp.dot(
                    jnp.concatenate(halves(wide), axis=0), T[r], preferred_element_type=jnp.float32
                )
                lap = (flat[: 4 * ORB] + flat[4 * ORB :]).reshape(4, ORB, 256)
                near = planes(src, src_off - 1, everything, lanes) + planes(src, src_off + 1, everything, lanes)
                far = planes(src, src_off - 2, everything, lanes) + planes(src, src_off + 2, everything, lanes)
                weight = planes(W, 4, everything, lanes)
                weight = jnp.concatenate([weight, weight, weight], axis=1)
                emit(lanes, NEAR * (lap + (16.0 * near - far)) + weight * v, v)
            return carry

        lax.fori_loop(0, 3, body, 0)

    def put(ref, off, starts, lanes, value):
        count = 4 // len(starts)
        for n, z in enumerate(starts):
            ref[pl.ds(z + off, count), :, lanes] = value[n * count : (n + 1) * count]

    def stage_s(*starts):
        def emit(lanes, h, v):
            put(S, 4, starts, lanes, h)

        stage(O, 6, starts, emit)

    def stage_f(*starts):
        count = 4 // len(starts)

        def emit(lanes, h, v):
            old = jnp.concatenate([O[pl.ds(z + 6, count), :, lanes] for z in starts], axis=0)
            put(F, 2, starts, lanes, 2.0 * h - old)

        stage(S, 4, starts, emit)

    def stage_a(*starts):
        def emit(lanes, h, v):
            put(A, 0, starts, lanes, HALF_WIDTH * h + CENTER * v)

        stage(F, 2, starts, emit)

    first = z_hi == 0

    def across(slot, row, piece):
        dst = RA_far.at[row] if slot == 3 else RF.at[slot, 1, row, core]
        return pltpu.make_async_remote_copy(
            src_ref=piece, dst_ref=dst,
            send_sem=far_s.at[slot, row], recv_sem=far_r.at[slot, row],
            device_id=to_band(1 - z_hi, y, core), device_id_type=MESH,
        )

    def sends_across(slot):
        return first if slot in (0, 3) else jnp.logical_not(first)

    def takes_across(slot):
        return jnp.logical_not(first) if slot in (0, 3) else first

    def landed(slot, row):
        return RA.at[0, row] if slot == 3 else RF.at[slot, 0, row, core]

    def swap(kind, q):
        src, off = ((F, 2), (A, 0))[kind]

        def part(row, n):
            plane = CHUNK_BASE[q] + row + CHUNK_STRIDE[q] * (row // 2)
            return src.at[plane + off, :, pl.ds(n * HALF, HALF)]

        def place(n):
            lanes = pl.ds(n * HALF, HALF)
            return RF.at[q, 0, y, core, :, lanes] if kind == 0 else RA.at[q, y, :, lanes]

        copies = []
        for n in range(2):
            for d in PEERS:
                row = (y + d) % 4
                copies.append(
                    send(part(row, n), place(n), swap_s.at[kind, q, d - 1, n], swap_r.at[kind, q, d - 1, n],
                         to_band(z_hi, row, core))
                )
        for n in range(2):
            own = pltpu.make_async_copy(part(y, n), place(n), own_sem.at[kind, q, n])
            own.start()
            copies.append(own)
        if kind == 0 or q == 0:
            slot = 3 if kind else q

            @pl.when(sends_across(slot))
            def _():
                plane = CHUNK_BASE[q] + y + CHUNK_STRIDE[q] * (y // 2)
                across(slot, y, src.at[plane + off]).start()

        return copies

    def swap_wait(copies):
        for copy in copies[:-2]:
            copy.wait_recv()
        for own in copies[-2:]:
            own.wait()

    def forward(q, half):
        piece = RF.at[q, half, :, core]
        return pltpu.make_async_remote_copy(
            src_ref=piece, dst_ref=piece, send_sem=fwd_s.at[q, half], recv_sem=fwd_r.at[q, half],
            device_id=to_band(z_hi, y, 1 - core), device_id_type=MESH,
        )

    def pass_on(slot, copies):
        for n, d in enumerate(PEERS):
            copies[n].wait_recv()
            copies[n + 3].wait_recv()

            @pl.when(sends_across(slot))
            def _():
                row = (y + 4 - d) % 4
                across(slot, row, landed(slot, row)).start()

        for own in copies[-2:]:
            own.wait()
        if slot < 3:
            forward(slot, 0).start()

    def wait_across(slot):
        for row in range(4):
            across(slot, row, landed(slot, row)).wait_recv()

    def pass_far(q):
        @pl.when(first)
        def _():
            wait_across(q)
            forward(q, 1).start()

    def gram(q, half, columns, f_rows, a_rows):
        def body(k, carry):
            lanes = pl.ds(pl.multiple_of(k * CHUNK, 128), CHUNK)
            f_high, f_low = halves(RF[q, columns, :, :, :, lanes].reshape(HALF_ORB, CHUNK))
            rows = jnp.concatenate([RF[q, f_rows, :, core, :, lanes], a_rows[:, :, lanes]], axis=0)
            high, low = halves(rows.reshape(2 * ROWS, CHUNK))
            both = dot_nt(jnp.concatenate([high, low], axis=0), f_high)
            part = (both[: 2 * ROWS] + both[2 * ROWS :]) + dot_nt(high, f_low)
            G[half] = G[half] + part.reshape(2, ROWS, HALF_ORB)
            return carry

        lax.fori_loop(0, NXY // CHUNK, body, 0)

    def gram_own(q):
        gram(q, 0, 0, 0, RA.at[q])

    def gram_far(q):
        @pl.when(first)
        def _():
            forward(q, 1).wait_recv()
            gram(q, 1, 1, 0, RA.at[q])

    def early():
        return pltpu.make_async_remote_copy(
            src_ref=G.at[1], dst_ref=G_far, send_sem=early_s, recv_sem=early_r,
            device_id=to_band(1 - z_hi, y, core), device_id_type=MESH,
        )

    def panel(row):
        return G.at[:, :, pl.ds(pl.multiple_of(row * ORB, 8), ORB)]

    def cross(row, side):
        index = row * 2 + side
        return pltpu.make_async_remote_copy(
            src_ref=XB.at[index], dst_ref=XR.at[y * 2 + core],
            send_sem=x_s.at[index], recv_sem=x_r.at[y * 2 + core],
            device_id=to_band(1 - z_hi, row, side), device_id_type=MESH,
        )

    def cross_from(index):
        return pltpu.make_async_remote_copy(
            src_ref=XB.at[index], dst_ref=XR.at[index],
            send_sem=x_s.at[index], recv_sem=x_r.at[index],
            device_id=to_band(1 - z_hi, index // 2, index % 2), device_id_type=MESH,
        )

    def reduce_band():
        copies = []
        for d in PEERS:
            row = (y + d) % 4
            copies.append(
                send(panel(row), R1.at[d - 1], r1_s.at[d - 1], r1_r.at[d - 1], to_band(z_hi, row, core))
            )

        @pl.when(first)
        def _():
            for kind in range(2):
                block = jnp.concatenate(
                    [G[1, kind], jnp.zeros((128 - ROWS, HALF_ORB), jnp.float32)], axis=0
                )
                XB[:, kind] = jnp.transpose(block).reshape(8, ORB, 128)
            for row in range(4):
                for side in range(2):
                    cross(row, side).start()

        return copies

    lane = lax.broadcasted_iota(jnp.int32, (ORB, 128), 1)

    def lanes_from(value, start):
        return pltpu.roll(value, (-start) % value.shape[1], 1)[:, :128]

    def reduce_slab(arrived):
        for copy in arrived:
            copy.wait_recv()
        mine = pl.ds(pl.multiple_of(y * ORB, 8), ORB)

        def rows_of(half, kind):
            rows = G[half, kind, mine]
            for d in range(len(PEERS)):
                rows = rows + R1[d, half, kind]
            return jnp.concatenate([rows, jnp.zeros((ORB, 64), jnp.float32)], axis=1)

        @pl.when(first)
        def _():
            for kind in range(2):
                own, other = rows_of(0, kind), rows_of(1, kind)
                for s in range(4):
                    B2[s, kind] = lanes_from(own, NX * s)
                    B2[s + 4, kind] = lanes_from(other, NX * s)

        @pl.when(jnp.logical_not(first))
        def _():
            for index in range(8):
                cross_from(index).wait_recv()
            for kind in range(2):
                own = rows_of(0, kind)
                sides = []
                for side in range(2):
                    total = XR[side, kind]
                    for row in range(1, 4):
                        total = total + XR[2 * row + side, kind]
                    sides.append(total)
                for s in range(4):
                    even = lanes_from(sides[0], ORB * s)
                    odd = pltpu.roll(sides[1], (ORB - ORB * s) % 128, 1)
                    B2[s, kind] = jnp.where(lane < ORB, even, odd)
                    B2[s + 4, kind] = lanes_from(own, NX * s)

        copies = []
        for d in range(1, SLABS):
            s = (slab + d) % SLABS
            copies.append(
                send(B2.at[s], R2.at[d - 1], r2_s.at[d - 1], r2_r.at[d - 1], to_slab(s))
            )
        return copies

    def finish(arrived):
        for copy in arrived:
            copy.wait_recv()
        for kind, out in enumerate((corr_ref, proj_ref)):
            block = B2[slab, kind]
            for d in range(SLABS - 1):
                block = block + R2[d, kind]
            out[...] = block[:, :NX] * (1.0 / CELLS)

    G[...] = jnp.zeros(G.shape, jnp.float32)
    stage_s(2)
    stage_s(6)
    stage_f(4)

    pl.semaphore_wait(barrier, len(partners))
    pots = [
        send(pot_ref.at[pl.ds(4, 8)], V_in.at[0], pot_s.at[0], pot_r.at[0], to_slab(up)),
        send(pot_ref.at[pl.ds(0, 8)], V_in.at[1], pot_s.at[1], pot_r.at[1], to_slab(down)),
    ]
    halos = []
    for t in range(3):
        halos.append((
            send(O.at[pl.ds(16 - 2 * t, 2)], O.at[pl.ds(4 - 2 * t, 2)],
                 halo_s.at[0, t], halo_r.at[0, t], to_slab(up)),
            send(O.at[pl.ds(6 + 2 * t, 2)], O.at[pl.ds(18 + 2 * t, 2)],
                 halo_s.at[1, t], halo_r.at[1, t], to_slab(down)),
        ))
    f0 = swap(0, 0)

    for copy in halos[0]:
        copy.wait_recv()
    stage_s(0, 10)
    stage_f(2, 8)
    f1 = swap(0, 1)
    stage_a(4)
    a0 = swap(1, 0)
    pass_on(0, f0)

    for copy in pots:
        copy.wait_recv()
    for n in range(4):
        fill(n - 4, V_in[0, 4 + n : 5 + n, :])
        fill(12 + n, V_in[1, n : n + 1, :])
    for copy in halos[1]:
        copy.wait_recv()
    stage_s(-2, 12)
    stage_f(0, 10)
    f2 = swap(0, 2)
    store = pltpu.make_async_copy(F.at[pl.ds(2, PLANES)], filt_hbm, out_sem)
    store.start()
    stage_a(2, 8)
    a1 = swap(1, 1)
    pass_on(1, f1)
    pass_on(3, a0)

    for copy in halos[2]:
        copy.wait_recv()
    stage_s(-4, 14)
    stage_f(-2, 12)
    stage_a(0, 10)
    a2 = swap(1, 2)
    pass_on(2, f2)

    forward(0, 0).wait_recv()
    gram_own(0)
    pass_far(1)

    @pl.when(jnp.logical_not(first))
    def _():
        wait_across(0)
        wait_across(3)
        gram(0, 1, 0, 1, RA_far)
        early().start()

    forward(1, 0).wait_recv()
    swap_wait(a1)
    gram_own(1)
    gram_far(1)
    pass_far(2)

    @pl.when(first)
    def _():
        early().wait_recv()
        G[1] = G[1] + G_far[...]

    forward(2, 0).wait_recv()
    swap_wait(a2)
    gram_own(2)
    gram_far(2)
    finish(reduce_slab(reduce_band()))

    for copy in sends:
        copy.wait_send()
    for q in range(3):
        forward(q, 0).wait_send()

    @pl.when(first)
    def _():
        for q in (1, 2):
            forward(q, 1).wait_send()
        for row in range(4):
            for side in range(2):
                cross(row, side).wait_send()
            across(0, row, landed(0, row)).wait_send()
            across(3, row, landed(3, row)).wait_send()

    @pl.when(jnp.logical_not(first))
    def _():
        for slot in (1, 2):
            for row in range(4):
                across(slot, row, landed(slot, row)).wait_send()
        early().wait_send()

    store.wait()


def local(orbitals, potential):
    f32 = jnp.float32
    dma = pltpu.SemaphoreType.DMA
    peers = len(PEERS)
    filtered, correlation, projected = pl.pallas_call(
        kernel,
        out_shape=(
            jax.ShapeDtypeStruct((PLANES, ORB, NXY), f32),
            jax.ShapeDtypeStruct((ORB, NX), f32),
            jax.ShapeDtypeStruct((ORB, NX), f32),
        ),
        in_specs=[
            pl.BlockSpec(memory_space=pl.ANY),
            pl.BlockSpec(memory_space=pltpu.VMEM),
            pl.BlockSpec(memory_space=pl.ANY),
        ],
        out_specs=(
            pl.BlockSpec(memory_space=pl.ANY),
            pl.BlockSpec(memory_space=pltpu.VMEM),
            pl.BlockSpec(memory_space=pltpu.VMEM),
        ),
        scratch_shapes=[
            pltpu.VMEM((PLANES + 12, ORB, NXY), f32),
            pltpu.VMEM((3, 512, 256), jnp.bfloat16),
            pltpu.VMEM((2, 8, NXY), f32),
            pltpu.VMEM((PLANES + 8, 8, NXY), f32),
            pltpu.VMEM((PLANES + 8, ORB, NXY), f32),
            pltpu.VMEM((PLANES + 4, ORB, NXY), f32),
            pltpu.VMEM((PLANES, ORB, NXY), f32),
            pltpu.VMEM((3, 2, 4, 2, ORB, NXY), f32),
            pltpu.VMEM((3, 4, ORB, NXY), f32),
            pltpu.VMEM((4, ORB, NXY), f32),
            pltpu.VMEM((2, 2, ROWS, HALF_ORB), f32),
            pltpu.VMEM((2, ROWS, HALF_ORB), f32),
            pltpu.VMEM((peers, 2, 2, ORB, HALF_ORB), f32),
            pltpu.VMEM((8, 2, ORB, 128), f32),
            pltpu.VMEM((8, 2, ORB, 128), f32),
            pltpu.VMEM((SLABS, 2, ORB, 128), f32),
            pltpu.VMEM((SLABS - 1, 2, ORB, 128), f32),
            dma, dma, dma,
            dma((2, 3)), dma((2, 3)),
            dma((2,)), dma((2,)),
            dma((2, 3, peers, 2)), dma((2, 3, peers, 2)),
            dma((2, 3, 2)),
            dma((3, 2)), dma((3, 2)),
            dma((4, 4)), dma((4, 4)),
            dma, dma,
            dma((peers,)), dma((peers,)),
            dma((8,)), dma((8,)),
            dma((SLABS - 1,)), dma((SLABS - 1,)),
        ],
        compiler_params=pltpu.CompilerParams(
            collective_id=0, has_side_effects=True, vmem_limit_bytes=56 << 20
        ),
        cost_estimate=pl.CostEstimate(
            flops=3_500_000_000, bytes_accessed=6_000_000, transcendentals=0
        ),
    )(jnp.transpose(orbitals, (1, 0, 2)), potential, plane_table())
    return jnp.transpose(filtered, (1, 0, 2)), correlation, projected


def solution(mesh):
    return jax.shard_map(
        local,
        mesh=mesh,
        in_specs=(P("band", "slab", None), P("slab", None)),
        out_specs=(P("band", "slab", None), P("band", "slab"), P("band", "slab")),
        check_vma=False,
    )
```

```python
import jax
import jax.numpy as jnp
import ml_dtypes
import numpy as np
from jax import lax
from jax.experimental import pallas as pl
from jax.experimental.pallas import tpu as pltpu
from jax.sharding import PartitionSpec as P

NX = 48
NXY = 2304
ORB = 24
PLANES = 12
SLABS = 8
HALF = NXY // 2
CHUNK = 384
CELLS = 221184

SPACING = 0.32
STENCIL = 1.0 / (12.0 * SPACING * SPACING)
CENTER = 38.0
HALF_WIDTH = 42.0
NEAR = -0.5 * STENCIL / HALF_WIDTH
MESH = pl.DeviceIdType.MESH

CHUNK_BASE = (4, 2, 0)
CHUNK_STRIDE = (0, 4, 8)
ENDS = (3, 0)
RELAYS = (1, 2)
PEERS = (1, 3, 2)
HALF_ORB = 192
ROWS = 96


def plane_table():
    table = np.zeros((3, 512, 256), np.float32)
    for r in range(3):
        for n in range(256):
            cell = 256 * r + n
            row, x = cell // NX, cell % NX
            for offset, weight in ((1, 16.0), (2, -1.0), (-1, 16.0), (-2, -1.0)):
                table[r, row * NX + (x + offset) % NX - 256 * r + 128, n] += weight
                table[r, n + 128 + offset * NX, n] += weight
    return table.astype(ml_dtypes.bfloat16)


def dot_nt(a, b):
    return lax.dot_general(a, b, (((1,), (1,)), ((), ())), preferred_element_type=jnp.float32)


def halves(a):
    high = a.astype(jnp.bfloat16)
    return high, (a - high.astype(jnp.float32)).astype(jnp.bfloat16)


def kernel(
    orb_hbm, pot_ref, table_hbm, filt_hbm, corr_ref, proj_ref,
    O, relay, T, V_in, W, S, F, A, RF, RA, RA_far, G, G_far, SB, R1, XB, XR, B2, R2,
    load_sem, table_sem, out_sem, halo_s, halo_r, relay_s, relay_r, pot_s, pot_r, swap_s, swap_r, own_sem, fwd_s, fwd_r,
    far_s, far_r, early_s, early_r, r1_s, r1_r, x_s, x_r, r2_s, r2_r,
):
    band, slab = lax.axis_index("band"), lax.axis_index("slab")
    chip, core = band // 2, band % 2
    z_hi, y = chip // 4, chip % 4

    def to_band(z, row, side):
        return {"band": z * 8 + row * 2 + side, "slab": slab}

    def to_slab(s):
        return {"band": band, "slab": s}

    load = pltpu.make_async_copy(orb_hbm, O.at[pl.ds(6, PLANES)], load_sem)
    load.start()
    table_load = pltpu.make_async_copy(table_hbm, T, table_sem)
    table_load.start()

    up, down = (slab + 1) % SLABS, (slab + SLABS - 1) % SLABS
    partners = [to_band(z_hi, (y + d) % 4, core) for d in PEERS]
    partners.append(to_band(z_hi, y, 1 - core))
    partners += [to_band(1 - z_hi, row, side) for row in range(4) for side in range(2)]
    partners += [to_slab((slab + d) % SLABS) for d in range(1, SLABS)]
    x_pos, z_lo = slab % 4, slab // 4

    def halo_copy(src, dst, s_sem, r_sem, where):
        return pltpu.make_async_remote_copy(
            src_ref=src, dst_ref=dst, send_sem=s_sem, recv_sem=r_sem,
            device_id=to_slab(where), device_id_type=MESH,
        )

    def outer(side):
        return O.at[pl.ds((12, 10)[side], 2)], O.at[pl.ds((0, 22)[side], 2)]

    def direct(side):
        src, dst = outer(side)
        return halo_copy(src, dst, halo_s.at[side, 2], halo_r.at[side, 2], (up, down)[side])

    def to_relay(side):
        return halo_copy(outer(side)[0], relay.at[side], halo_s.at[side, 2], relay_r.at[side],
                         (1 - z_lo) * 4 + RELAYS[side])

    def from_relay(side):
        return halo_copy(relay.at[side], outer(side)[1], relay_s.at[side], halo_r.at[side, 2],
                         z_lo * 4 + ENDS[1 - side])

    def pass_halo():
        for side in range(2):

            @pl.when(x_pos == RELAYS[side])
            def _():
                to_relay(side).wait_recv()
                from_relay(side).start()

    barrier = pltpu.get_barrier_semaphore()
    for partner in partners:
        pl.semaphore_signal(barrier, inc=1, device_id=partner, device_id_type=MESH)

    sends = []

    def send(src, dst, s_sem, r_sem, where):
        copy = pltpu.make_async_remote_copy(
            src_ref=src, dst_ref=dst, send_sem=s_sem, recv_sem=r_sem,
            device_id=where, device_id_type=MESH,
        )
        copy.start()
        sends.append(copy)
        return copy

    def fill(z, row):
        weight = (row + (45.0 * STENCIL - CENTER)) * (1.0 / HALF_WIDTH)
        W[z + 4] = jnp.broadcast_to(weight, (8, NXY))

    for z in range(PLANES):
        fill(z, pot_ref[z : z + 1, :])

    table_load.wait()
    load.wait()

    def stage(src, src_off, starts, emit):
        count = 4 // len(starts)

        def planes(ref, off, rows, lanes):
            parts = [ref[pl.ds(z + off, count), rows, lanes] for z in starts]
            return parts[0] if len(parts) == 1 else jnp.concatenate(parts, axis=0)

        everything = slice(None)

        def body(i, carry):
            for r in range(3):
                base = i * 768 + 256 * r
                lanes = pl.ds(pl.multiple_of(base, 128), 256)
                left = pl.ds(pl.multiple_of((base + NXY - 128) % NXY, 128), 128)
                right = pl.ds(pl.multiple_of((base + 256) % NXY, 128), 128)
                v = planes(src, src_off, everything, lanes)
                wide = jnp.concatenate(
                    [planes(src, src_off, everything, left), v, planes(src, src_off, everything, right)],
                    axis=2,
                ).reshape(4 * ORB, 512)
                flat = jnp.dot(
                    jnp.concatenate(halves(wide), axis=0), T[r], preferred_element_type=jnp.float32
                )
                lap = (flat[: 4 * ORB] + flat[4 * ORB :]).reshape(4, ORB, 256)
                near = planes(src, src_off - 1, everything, lanes) + planes(src, src_off + 1, everything, lanes)
                far = planes(src, src_off - 2, everything, lanes) + planes(src, src_off + 2, everything, lanes)
                weight = planes(W, 4, everything, lanes)
                weight = jnp.concatenate([weight, weight, weight], axis=1)
                emit(lanes, NEAR * (lap + (16.0 * near - far)) + weight * v, v)
            return carry

        lax.fori_loop(0, 3, body, 0)

    def put(ref, off, starts, lanes, value):
        count = 4 // len(starts)
        for n, z in enumerate(starts):
            ref[pl.ds(z + off, count), :, lanes] = value[n * count : (n + 1) * count]

    def stage_s(*starts):
        def emit(lanes, h, v):
            put(S, 4, starts, lanes, h)

        stage(O, 6, starts, emit)

    def stage_f(*starts):
        count = 4 // len(starts)

        def emit(lanes, h, v):
            old = jnp.concatenate([O[pl.ds(z + 6, count), :, lanes] for z in starts], axis=0)
            put(F, 2, starts, lanes, 2.0 * h - old)

        stage(S, 4, starts, emit)

    def stage_a(*starts):
        def emit(lanes, h, v):
            put(A, 0, starts, lanes, HALF_WIDTH * h + CENTER * v)

        stage(F, 2, starts, emit)

    first = z_hi == 0

    def across(slot, row, piece):
        dst = RA_far.at[row] if slot == 3 else RF.at[slot, 1, row, core]
        return pltpu.make_async_remote_copy(
            src_ref=piece, dst_ref=dst,
            send_sem=far_s.at[slot, row], recv_sem=far_r.at[slot, row],
            device_id=to_band(1 - z_hi, y, core), device_id_type=MESH,
        )

    def sends_across(slot):
        return first if slot in (0, 3) else jnp.logical_not(first)

    def takes_across(slot):
        return jnp.logical_not(first) if slot in (0, 3) else first

    def landed(slot, row):
        return RA.at[0, row] if slot == 3 else RF.at[slot, 0, row, core]

    def swap(kind, q):
        src, off = ((F, 2), (A, 0))[kind]

        def part(row, n):
            plane = CHUNK_BASE[q] + row + CHUNK_STRIDE[q] * (row // 2)
            return src.at[plane + off, :, pl.ds(n * HALF, HALF)]

        def place(n):
            lanes = pl.ds(n * HALF, HALF)
            return RF.at[q, 0, y, core, :, lanes] if kind == 0 else RA.at[q, y, :, lanes]

        copies = []
        for n in range(2):
            for d in PEERS:
                row = (y + d) % 4
                copies.append(
                    send(part(row, n), place(n), swap_s.at[kind, q, d - 1, n], swap_r.at[kind, q, d - 1, n],
                         to_band(z_hi, row, core))
                )
        for n in range(2):
            own = pltpu.make_async_copy(part(y, n), place(n), own_sem.at[kind, q, n])
            own.start()
            copies.append(own)
        if kind == 0 or q == 0:
            slot = 3 if kind else q

            @pl.when(sends_across(slot))
            def _():
                plane = CHUNK_BASE[q] + y + CHUNK_STRIDE[q] * (y // 2)
                across(slot, y, src.at[plane + off]).start()

        return copies

    def swap_wait(copies):
        for copy in copies[:-2]:
            copy.wait_recv()
        for own in copies[-2:]:
            own.wait()

    def forward(q, half):
        piece = RF.at[q, half, :, core]
        return pltpu.make_async_remote_copy(
            src_ref=piece, dst_ref=piece, send_sem=fwd_s.at[q, half], recv_sem=fwd_r.at[q, half],
            device_id=to_band(z_hi, y, 1 - core), device_id_type=MESH,
        )

    def pass_on(slot, copies):
        for n, d in enumerate(PEERS):
            copies[n].wait_recv()
            copies[n + 3].wait_recv()

            @pl.when(sends_across(slot))
            def _():
                row = (y + 4 - d) % 4
                across(slot, row, landed(slot, row)).start()

        for own in copies[-2:]:
            own.wait()
        if slot < 3:
            forward(slot, 0).start()

    def wait_across(slot):
        for row in range(4):
            across(slot, row, landed(slot, row)).wait_recv()

    def pass_far(q):
        @pl.when(first)
        def _():
            wait_across(q)
            forward(q, 1).start()

    def gram(q, half, columns, f_rows, a_rows, kinds=(0, 1)):
        count = len(kinds) * ROWS

        def body(k, carry):
            lanes = pl.ds(pl.multiple_of(k * CHUNK, 128), CHUNK)
            f_high, f_low = halves(RF[q, columns, :, :, :, lanes].reshape(HALF_ORB, CHUNK))
            rows = [RF[q, f_rows, :, core, :, lanes] if kind == 0 else a_rows[:, :, lanes] for kind in kinds]
            rows = rows[0] if len(kinds) == 1 else jnp.concatenate(rows, axis=0)
            high, low = halves(rows.reshape(count, CHUNK))
            both = dot_nt(jnp.concatenate([high, low], axis=0), f_high)
            part = (both[:count] + both[count:]) + dot_nt(high, f_low)
            for n, kind in enumerate(kinds):
                G[half, kind] = G[half, kind] + part[n * ROWS : (n + 1) * ROWS]
            return carry

        lax.fori_loop(0, NXY // CHUNK, body, 0)

    def gram_own(q, kinds=(0, 1)):
        gram(q, 0, 0, 0, RA.at[q], kinds)

    def gram_far(q, kinds=(0, 1), wait=True):
        @pl.when(first)
        def _():
            if wait:
                forward(q, 1).wait_recv()
            gram(q, 1, 1, 0, RA.at[q], kinds)

    def early():
        return pltpu.make_async_remote_copy(
            src_ref=G.at[1], dst_ref=G_far, send_sem=early_s, recv_sem=early_r,
            device_id=to_band(1 - z_hi, y, core), device_id_type=MESH,
        )

    def to_row(kind, d, width):
        row = (y + d) % 4
        return pltpu.make_async_remote_copy(
            src_ref=SB.at[kind, pl.ds(pl.multiple_of(row * ORB, 8), ORB), pl.ds(0, width)],
            dst_ref=R1.at[kind, d - 1, :, pl.ds(0, width)],
            send_sem=r1_s.at[kind, d - 1], recv_sem=r1_r.at[kind, d - 1],
            device_id=to_band(z_hi, row, core), device_id_type=MESH,
        )

    def cross(kind, row, side):
        index = row * 2 + side
        return pltpu.make_async_remote_copy(
            src_ref=XB.at[kind, index], dst_ref=XR.at[kind, y * 2 + core],
            send_sem=x_s.at[kind, index], recv_sem=x_r.at[kind, y * 2 + core],
            device_id=to_band(1 - z_hi, row, side), device_id_type=MESH,
        )

    def cross_from(kind, index):
        return pltpu.make_async_remote_copy(
            src_ref=XB.at[kind, index], dst_ref=XR.at[kind, index],
            send_sem=x_s.at[kind, index], recv_sem=x_r.at[kind, index],
            device_id=to_band(1 - z_hi, index // 2, index % 2), device_id_type=MESH,
        )

    def reduce_band(kind):
        SB[kind] = jnp.concatenate([G[0, kind], G[1, kind]], axis=1)

        @pl.when(first)
        def _():
            for d in PEERS:
                to_row(kind, d, 384).start()
            block = jnp.concatenate([G[1, kind], jnp.zeros((128 - ROWS, HALF_ORB), jnp.float32)], axis=0)
            XB[kind] = jnp.transpose(block).reshape(8, ORB, 128)
            for row in range(4):
                for side in range(2):
                    cross(kind, row, side).start()

        @pl.when(jnp.logical_not(first))
        def _():
            for d in PEERS:
                to_row(kind, d, 256).start()

    lane = lax.broadcasted_iota(jnp.int32, (ORB, 128), 1)

    def lanes_from(value, start):
        return pltpu.roll(value, (-start) % value.shape[1], 1)[:, :128]

    def reduce_rows(kind):
        mine = pl.ds(pl.multiple_of(y * ORB, 8), ORB)

        @pl.when(first)
        def _():
            rows = SB[kind, mine]
            for d in PEERS:
                to_row(kind, d, 384).wait_recv()
                rows = rows + R1[kind, d - 1]
            for s in range(SLABS):
                B2[s, kind] = lanes_from(rows, NX * s)

        @pl.when(jnp.logical_not(first))
        def _():
            rows = SB[kind, mine, pl.ds(0, 256)]
            for d in PEERS:
                to_row(kind, d, 256).wait_recv()
                rows = rows + R1[kind, d - 1, :, pl.ds(0, 256)]
            for index in range(8):
                cross_from(kind, index).wait_recv()
            sides = []
            for side in range(2):
                total = XR[kind, side]
                for row in range(1, 4):
                    total = total + XR[kind, 2 * row + side]
                sides.append(total)
            for s in range(4):
                even = lanes_from(sides[0], ORB * s)
                odd = pltpu.roll(sides[1], (ORB - ORB * s) % 128, 1)
                B2[s, kind] = jnp.where(lane < ORB, even, odd)
                B2[s + 4, kind] = lanes_from(rows, NX * s)

    def reduce_slab():
        copies = []
        for d in range(1, SLABS):
            s = (slab + d) % SLABS
            copies.append(
                send(B2.at[s], R2.at[d - 1], r2_s.at[d - 1], r2_r.at[d - 1], to_slab(s))
            )
        return copies

    def finish(arrived):
        for copy in arrived:
            copy.wait_recv()
        for kind, out in enumerate((corr_ref, proj_ref)):
            block = B2[slab, kind]
            for d in range(SLABS - 1):
                block = block + R2[d, kind]
            out[...] = block[:, :NX] * (1.0 / CELLS)

    G[...] = jnp.zeros(G.shape, jnp.float32)
    stage_s(2)
    stage_s(6)
    stage_f(4)

    pl.semaphore_wait(barrier, len(partners))
    pots = [
        send(pot_ref.at[pl.ds(4, 8)], V_in.at[0], pot_s.at[0], pot_r.at[0], to_slab(up)),
        send(pot_ref.at[pl.ds(0, 8)], V_in.at[1], pot_s.at[1], pot_r.at[1], to_slab(down)),
    ]
    halos = []
    for t in range(2):
        halos.append((
            send(O.at[pl.ds(16 - 2 * t, 2)], O.at[pl.ds(4 - 2 * t, 2)],
                 halo_s.at[0, t], halo_r.at[0, t], to_slab(up)),
            send(O.at[pl.ds(6 + 2 * t, 2)], O.at[pl.ds(18 + 2 * t, 2)],
                 halo_s.at[1, t], halo_r.at[1, t], to_slab(down)),
        ))
    for side in range(2):

        @pl.when(x_pos == ENDS[side])
        def _():
            to_relay(side).start()

        @pl.when(x_pos != ENDS[side])
        def _():
            direct(side).start()

    f0 = swap(0, 0)

    for copy in halos[0]:
        copy.wait_recv()
    stage_s(0, 10)
    stage_f(2, 8)
    f1 = swap(0, 1)
    stage_a(4)
    a0 = swap(1, 0)
    pass_on(0, f0)

    for copy in pots:
        copy.wait_recv()
    for n in range(4):
        fill(n - 4, V_in[0, 4 + n : 5 + n, :])
        fill(12 + n, V_in[1, n : n + 1, :])
    for copy in halos[1]:
        copy.wait_recv()
    stage_s(-2, 12)
    stage_f(0, 10)
    f2 = swap(0, 2)
    store = pltpu.make_async_copy(F.at[pl.ds(2, PLANES)], filt_hbm, out_sem)
    store.start()
    stage_a(2, 8)
    a1 = swap(1, 1)
    pass_on(1, f1)
    pass_halo()

    for side in range(2):
        direct(side).wait_recv()
    stage_s(-4, 14)
    stage_f(-2, 12)
    stage_a(0, 10)
    a2 = swap(1, 2)
    pass_on(3, a0)
    pass_on(2, f2)

    forward(0, 0).wait_recv()
    gram_own(0)
    pass_far(1)

    @pl.when(jnp.logical_not(first))
    def _():
        wait_across(0)
        wait_across(3)
        gram(0, 1, 0, 1, RA_far)
        early().start()

    forward(1, 0).wait_recv()
    swap_wait(a1)
    gram_own(1)
    gram_far(1)
    forward(2, 0).wait_recv()
    gram_own(2, (0,))
    pass_far(2)

    @pl.when(first)
    def _():
        early().wait_recv()
        G[1] = G[1] + G_far[...]

    gram_far(2, (0,))
    reduce_band(0)
    swap_wait(a2)
    gram_own(2, (1,))
    gram_far(2, (1,), False)
    reduce_band(1)
    reduce_rows(0)
    reduce_rows(1)
    finish(reduce_slab())

    for copy in sends:
        copy.wait_send()
    for side in range(2):
        direct(side).wait_send()

        @pl.when(x_pos == RELAYS[side])
        def _():
            from_relay(side).wait_send()

    for q in range(3):
        forward(q, 0).wait_send()

    @pl.when(first)
    def _():
        for q in (1, 2):
            forward(q, 1).wait_send()
        for kind in range(2):
            for d in PEERS:
                to_row(kind, d, 384).wait_send()
            for row in range(4):
                for side in range(2):
                    cross(kind, row, side).wait_send()
        for row in range(4):
            across(0, row, landed(0, row)).wait_send()
            across(3, row, landed(3, row)).wait_send()

    @pl.when(jnp.logical_not(first))
    def _():
        for slot in (1, 2):
            for row in range(4):
                across(slot, row, landed(slot, row)).wait_send()
        early().wait_send()
        for kind in range(2):
            for d in PEERS:
                to_row(kind, d, 256).wait_send()

    store.wait()


def local(orbitals, potential):
    f32 = jnp.float32
    dma = pltpu.SemaphoreType.DMA
    peers = len(PEERS)
    shapes = (
        pltpu.VMEM((PLANES, ORB, NXY), f32),
        pltpu.VMEM((ORB, NX), f32),
        pltpu.VMEM((ORB, NX), f32),
    )
    results = pl.pallas_call(
        kernel,
        out_shape=shapes,
        in_specs=[
            pl.BlockSpec(memory_space=pl.ANY),
            pl.BlockSpec(memory_space=pltpu.VMEM),
            pl.BlockSpec(memory_space=pl.ANY),
        ],
        out_specs=(
            pl.BlockSpec(memory_space=pltpu.VMEM),
            pl.BlockSpec(memory_space=pltpu.VMEM),
            pl.BlockSpec(memory_space=pltpu.VMEM),
        ),
        scratch_shapes=[
            pltpu.VMEM((PLANES + 12, ORB, NXY), f32),
            pltpu.VMEM((2, 2, ORB, NXY), f32),
            pltpu.VMEM((3, 512, 256), jnp.bfloat16),
            pltpu.VMEM((2, 8, NXY), f32),
            pltpu.VMEM((PLANES + 8, 8, NXY), f32),
            pltpu.VMEM((PLANES + 8, ORB, NXY), f32),
            pltpu.VMEM((PLANES + 4, ORB, NXY), f32),
            pltpu.VMEM((PLANES, ORB, NXY), f32),
            pltpu.VMEM((3, 2, 4, 2, ORB, NXY), f32),
            pltpu.VMEM((3, 4, ORB, NXY), f32),
            pltpu.VMEM((4, ORB, NXY), f32),
            pltpu.VMEM((2, 2, ROWS, HALF_ORB), f32),
            pltpu.VMEM((2, ROWS, HALF_ORB), f32),
            pltpu.VMEM((2, ROWS, 2 * HALF_ORB), f32),
            pltpu.VMEM((2, peers, ORB, 2 * HALF_ORB), f32),
            pltpu.VMEM((2, 8, ORB, 128), f32),
            pltpu.VMEM((2, 8, ORB, 128), f32),
            pltpu.VMEM((SLABS, 2, ORB, 128), f32),
            pltpu.VMEM((SLABS - 1, 2, ORB, 128), f32),
            dma, dma, dma,
            dma((2, 3)), dma((2, 3)),
            dma((2,)), dma((2,)),
            dma((2,)), dma((2,)),
            dma((2, 3, peers, 2)), dma((2, 3, peers, 2)),
            dma((2, 3, 2)),
            dma((3, 2)), dma((3, 2)),
            dma((4, 4)), dma((4, 4)),
            dma, dma,
            dma((2, peers)), dma((2, peers)),
            dma((2, 8)), dma((2, 8)),
            dma((SLABS - 1,)), dma((SLABS - 1,)),
        ],
        compiler_params=pltpu.CompilerParams(
            collective_id=0, has_side_effects=True, vmem_limit_bytes=56 << 20
        ),
        cost_estimate=pl.CostEstimate(
            flops=3_500_000_000, bytes_accessed=6_000_000, transcendentals=0
        ),
    )(jnp.transpose(orbitals, (1, 0, 2)), potential, plane_table())
    filtered, correlation, projected = results
    return jnp.transpose(filtered, (1, 0, 2)), correlation, projected


def solution(mesh):
    return jax.shard_map(
        local,
        mesh=mesh,
        in_specs=(P("band", "slab", None), P("slab", None)),
        out_specs=(P("band", "slab", None), P("band", "slab"), P("band", "slab")),
        check_vma=False,
    )
```

```python
import jax
import jax.numpy as jnp
import ml_dtypes
import numpy as np
from jax import lax
from jax.experimental import pallas as pl
from jax.experimental.pallas import tpu as pltpu
from jax.sharding import PartitionSpec as P

NX = 48
NXY = 2304
ORB = 24
PLANES = 12
SLABS = 8
HALF = NXY // 2
CHUNK = 384
CELLS = 221184

SPACING = 0.32
STENCIL = 1.0 / (12.0 * SPACING * SPACING)
CENTER = 38.0
HALF_WIDTH = 42.0
NEAR = -0.5 * STENCIL / HALF_WIDTH
MESH = pl.DeviceIdType.MESH

CHUNK_BASE = (4, 2, 0)
CHUNK_STRIDE = (0, 4, 8)
ENDS = (3, 0)
RELAYS = (1, 2)
PEERS = (1, 3, 2)
HALF_ORB = 192
ROWS = 96


def plane_table():
    table = np.zeros((3, 512, 256), np.float32)
    for r in range(3):
        for n in range(256):
            cell = 256 * r + n
            row, x = cell // NX, cell % NX
            for offset, weight in ((1, 16.0), (2, -1.0), (-1, 16.0), (-2, -1.0)):
                table[r, row * NX + (x + offset) % NX - 256 * r + 128, n] += weight
                table[r, n + 128 + offset * NX, n] += weight
    return table.astype(ml_dtypes.bfloat16)


def dot_nt(a, b):
    return lax.dot_general(a, b, (((1,), (1,)), ((), ())), preferred_element_type=jnp.float32)


def halves(a):
    high = a.astype(jnp.bfloat16)
    return high, (a - high.astype(jnp.float32)).astype(jnp.bfloat16)


def kernel(
    orb_hbm, pot_ref, table_hbm, filt_hbm, corr_ref, proj_ref,
    O, relay, T, V_in, W, S, F, A, RF, RA, RA_far, G, G_far, SB, R1, XB, XR, B2, R2,
    load_sem, table_sem, out_sem, halo_s, halo_r, relay_s, relay_r, pot_s, pot_r, swap_s, swap_r, own_sem, fwd_s, fwd_r,
    far_s, far_r, early_s, early_r, r1_s, r1_r, x_s, x_r, r2_s, r2_r,
):
    band, slab = lax.axis_index("band"), lax.axis_index("slab")
    chip, core = band // 2, band % 2
    z_hi, y = chip // 4, chip % 4

    def to_band(z, row, side):
        return {"band": z * 8 + row * 2 + side, "slab": slab}

    def to_slab(s):
        return {"band": band, "slab": s}

    load = pltpu.make_async_copy(orb_hbm, O.at[pl.ds(6, PLANES)], load_sem)
    load.start()
    table_load = pltpu.make_async_copy(table_hbm, T, table_sem)
    table_load.start()

    up, down = (slab + 1) % SLABS, (slab + SLABS - 1) % SLABS
    partners = [to_band(z_hi, (y + d) % 4, core) for d in PEERS]
    partners.append(to_band(z_hi, y, 1 - core))
    partners += [to_band(1 - z_hi, row, side) for row in range(4) for side in range(2)]
    partners += [to_slab((slab + d) % SLABS) for d in range(1, SLABS)]
    x_pos, z_lo = slab % 4, slab // 4

    def halo_copy(src, dst, s_sem, r_sem, where):
        return pltpu.make_async_remote_copy(
            src_ref=src, dst_ref=dst, send_sem=s_sem, recv_sem=r_sem,
            device_id=to_slab(where), device_id_type=MESH,
        )

    def outer(side):
        return O.at[pl.ds((12, 10)[side], 2)], O.at[pl.ds((0, 22)[side], 2)]

    def direct(side):
        src, dst = outer(side)
        return halo_copy(src, dst, halo_s.at[side, 2], halo_r.at[side, 2], (up, down)[side])

    def to_relay(side):
        return halo_copy(outer(side)[0], relay.at[side], halo_s.at[side, 2], relay_r.at[side],
                         (1 - z_lo) * 4 + RELAYS[side])

    def from_relay(side):
        return halo_copy(relay.at[side], outer(side)[1], relay_s.at[side], halo_r.at[side, 2],
                         z_lo * 4 + ENDS[1 - side])

    def pass_halo():
        for side in range(2):

            @pl.when(x_pos == RELAYS[side])
            def _():
                to_relay(side).wait_recv()
                from_relay(side).start()

    barrier = pltpu.get_barrier_semaphore()
    for partner in partners:
        pl.semaphore_signal(barrier, inc=1, device_id=partner, device_id_type=MESH)

    sends = []

    def send(src, dst, s_sem, r_sem, where):
        copy = pltpu.make_async_remote_copy(
            src_ref=src, dst_ref=dst, send_sem=s_sem, recv_sem=r_sem,
            device_id=where, device_id_type=MESH,
        )
        copy.start()
        sends.append(copy)
        return copy

    def fill(z, row):
        weight = (row + (45.0 * STENCIL - CENTER)) * (1.0 / HALF_WIDTH)
        W[z + 4] = jnp.broadcast_to(weight, (8, NXY))

    for z in range(PLANES):
        fill(z, pot_ref[z : z + 1, :])

    table_load.wait()
    load.wait()

    def stage(src, src_off, starts, emit):
        count = 4 // len(starts)

        def planes(ref, off, rows, lanes):
            parts = [ref[pl.ds(z + off, count), rows, lanes] for z in starts]
            return parts[0] if len(parts) == 1 else jnp.concatenate(parts, axis=0)

        everything = slice(None)

        def body(i, carry):
            for r in range(3):
                base = i * 768 + 256 * r
                lanes = pl.ds(pl.multiple_of(base, 128), 256)
                left = pl.ds(pl.multiple_of((base + NXY - 128) % NXY, 128), 128)
                right = pl.ds(pl.multiple_of((base + 256) % NXY, 128), 128)
                v = planes(src, src_off, everything, lanes)
                wide = jnp.concatenate(
                    [planes(src, src_off, everything, left), v, planes(src, src_off, everything, right)],
                    axis=2,
                ).reshape(4 * ORB, 512)
                flat = jnp.dot(
                    jnp.concatenate(halves(wide), axis=0), T[r], preferred_element_type=jnp.float32
                )
                lap = (flat[: 4 * ORB] + flat[4 * ORB :]).reshape(4, ORB, 256)
                near = planes(src, src_off - 1, everything, lanes) + planes(src, src_off + 1, everything, lanes)
                far = planes(src, src_off - 2, everything, lanes) + planes(src, src_off + 2, everything, lanes)
                weight = planes(W, 4, everything, lanes)
                weight = jnp.concatenate([weight, weight, weight], axis=1)
                emit(lanes, NEAR * (lap + (16.0 * near - far)) + weight * v, v)
            return carry

        lax.fori_loop(0, 3, body, 0)

    def put(ref, off, starts, lanes, value):
        count = 4 // len(starts)
        for n, z in enumerate(starts):
            ref[pl.ds(z + off, count), :, lanes] = value[n * count : (n + 1) * count]

    def stage_s(*starts):
        def emit(lanes, h, v):
            put(S, 4, starts, lanes, h)

        stage(O, 6, starts, emit)

    def stage_f(*starts):
        count = 4 // len(starts)

        def emit(lanes, h, v):
            old = jnp.concatenate([O[pl.ds(z + 6, count), :, lanes] for z in starts], axis=0)
            put(F, 2, starts, lanes, 2.0 * h - old)

        stage(S, 4, starts, emit)

    def stage_a(*starts):
        def emit(lanes, h, v):
            put(A, 0, starts, lanes, HALF_WIDTH * h + CENTER * v)

        stage(F, 2, starts, emit)

    first = z_hi == 0

    def across(slot, row, piece):
        dst = RA_far.at[row] if slot == 3 else RF.at[slot, 1, row, core]
        return pltpu.make_async_remote_copy(
            src_ref=piece, dst_ref=dst,
            send_sem=far_s.at[slot, row], recv_sem=far_r.at[slot, row],
            device_id=to_band(1 - z_hi, y, core), device_id_type=MESH,
        )

    def sends_across(slot):
        return first if slot in (0, 3) else jnp.logical_not(first)

    def takes_across(slot):
        return jnp.logical_not(first) if slot in (0, 3) else first

    def landed(slot, row):
        return RA.at[0, row] if slot == 3 else RF.at[slot, 0, row, core]

    def swap(kind, q):
        src, off = ((F, 2), (A, 0))[kind]

        def part(row, n):
            plane = CHUNK_BASE[q] + row + CHUNK_STRIDE[q] * (row // 2)
            return src.at[plane + off, :, pl.ds(n * HALF, HALF)]

        def place(n):
            lanes = pl.ds(n * HALF, HALF)
            return RF.at[q, 0, y, core, :, lanes] if kind == 0 else RA.at[q, y, :, lanes]

        copies = []
        for n in range(2):
            for d in PEERS:
                row = (y + d) % 4
                copies.append(
                    send(part(row, n), place(n), swap_s.at[kind, q, d - 1, n], swap_r.at[kind, q, d - 1, n],
                         to_band(z_hi, row, core))
                )
        for n in range(2):
            own = pltpu.make_async_copy(part(y, n), place(n), own_sem.at[kind, q, n])
            own.start()
            copies.append(own)
        if kind == 0 or q == 0:
            slot = 3 if kind else q

            @pl.when(sends_across(slot))
            def _():
                plane = CHUNK_BASE[q] + y + CHUNK_STRIDE[q] * (y // 2)
                across(slot, y, src.at[plane + off]).start()

        return copies

    def swap_wait(copies):
        for copy in copies[:-2]:
            copy.wait_recv()
        for own in copies[-2:]:
            own.wait()

    def forward(q, half):
        piece = RF.at[q, half, :, core]
        return pltpu.make_async_remote_copy(
            src_ref=piece, dst_ref=piece, send_sem=fwd_s.at[q, half], recv_sem=fwd_r.at[q, half],
            device_id=to_band(z_hi, y, 1 - core), device_id_type=MESH,
        )

    def pass_on(slot, copies):
        for n, d in enumerate(PEERS):
            copies[n].wait_recv()
            copies[n + 3].wait_recv()

            @pl.when(sends_across(slot))
            def _():
                row = (y + 4 - d) % 4
                across(slot, row, landed(slot, row)).start()

        for own in copies[-2:]:
            own.wait()
        if slot < 3:
            forward(slot, 0).start()

    def wait_across(slot):
        for row in range(4):
            across(slot, row, landed(slot, row)).wait_recv()

    def pass_far(q):
        @pl.when(first)
        def _():
            wait_across(q)
            forward(q, 1).start()

    def gram(q, half, columns, f_rows, a_rows, kinds=(0, 1)):
        count = len(kinds) * ROWS

        def body(k, carry):
            lanes = pl.ds(pl.multiple_of(k * 1152, 128), 1152)
            f_high, f_low = halves(RF[q, columns, :, :, :, lanes].reshape(HALF_ORB, 1152))
            rows = [RF[q, f_rows, :, core, :, lanes] if kind == 0 else a_rows[:, :, lanes] for kind in kinds]
            rows = rows[0] if len(kinds) == 1 else jnp.concatenate(rows, axis=0)
            high, low = halves(rows.reshape(count, 1152))
            both = dot_nt(jnp.concatenate([high, low], axis=0), f_high)
            part = (both[:count] + both[count:]) + dot_nt(high, f_low)
            for n, kind in enumerate(kinds):
                G[half, kind] = G[half, kind] + part[n * ROWS : (n + 1) * ROWS]
            return carry

        lax.fori_loop(0, NXY // 1152, body, 0)

    def gram_own(q, kinds=(0, 1)):
        gram(q, 0, 0, 0, RA.at[q], kinds)

    def gram_far(q, kinds=(0, 1), wait=True):
        @pl.when(first)
        def _():
            if wait:
                forward(q, 1).wait_recv()
            gram(q, 1, 1, 0, RA.at[q], kinds)

    def early():
        return pltpu.make_async_remote_copy(
            src_ref=G.at[1], dst_ref=G_far, send_sem=early_s, recv_sem=early_r,
            device_id=to_band(1 - z_hi, y, core), device_id_type=MESH,
        )

    def to_row(kind, d, width):
        row = (y + d) % 4
        return pltpu.make_async_remote_copy(
            src_ref=SB.at[kind, pl.ds(pl.multiple_of(row * ORB, 8), ORB), pl.ds(0, width)],
            dst_ref=R1.at[kind, d - 1, :, pl.ds(0, width)],
            send_sem=r1_s.at[kind, d - 1], recv_sem=r1_r.at[kind, d - 1],
            device_id=to_band(z_hi, row, core), device_id_type=MESH,
        )

    def cross(kind, row, side):
        index = row * 2 + side
        return pltpu.make_async_remote_copy(
            src_ref=XB.at[kind, index], dst_ref=XR.at[kind, y * 2 + core],
            send_sem=x_s.at[kind, index], recv_sem=x_r.at[kind, y * 2 + core],
            device_id=to_band(1 - z_hi, row, side), device_id_type=MESH,
        )

    def cross_from(kind, index):
        return pltpu.make_async_remote_copy(
            src_ref=XB.at[kind, index], dst_ref=XR.at[kind, index],
            send_sem=x_s.at[kind, index], recv_sem=x_r.at[kind, index],
            device_id=to_band(1 - z_hi, index // 2, index % 2), device_id_type=MESH,
        )

    def reduce_band(kind):
        SB[kind] = jnp.concatenate([G[0, kind], G[1, kind]], axis=1)

        @pl.when(first)
        def _():
            for d in PEERS:
                to_row(kind, d, 384).start()
            block = jnp.concatenate([G[1, kind], jnp.zeros((128 - ROWS, HALF_ORB), jnp.float32)], axis=0)
            XB[kind] = jnp.transpose(block).reshape(8, ORB, 128)
            for row in range(4):
                for side in range(2):
                    cross(kind, row, side).start()

        @pl.when(jnp.logical_not(first))
        def _():
            for d in PEERS:
                to_row(kind, d, 256).start()

    lane = lax.broadcasted_iota(jnp.int32, (ORB, 128), 1)

    def lanes_from(value, start):
        return pltpu.roll(value, (-start) % value.shape[1], 1)[:, :128]

    def reduce_rows(kind):
        mine = pl.ds(pl.multiple_of(y * ORB, 8), ORB)

        @pl.when(first)
        def _():
            rows = SB[kind, mine]
            for d in PEERS:
                to_row(kind, d, 384).wait_recv()
                rows = rows + R1[kind, d - 1]
            for s in range(SLABS):
                B2[s, kind] = lanes_from(rows, NX * s)

        @pl.when(jnp.logical_not(first))
        def _():
            rows = SB[kind, mine, pl.ds(0, 256)]
            for d in PEERS:
                to_row(kind, d, 256).wait_recv()
                rows = rows + R1[kind, d - 1, :, pl.ds(0, 256)]
            for index in range(8):
                cross_from(kind, index).wait_recv()
            sides = []
            for side in range(2):
                total = XR[kind, side]
                for row in range(1, 4):
                    total = total + XR[kind, 2 * row + side]
                sides.append(total)
            for s in range(4):
                even = lanes_from(sides[0], ORB * s)
                odd = pltpu.roll(sides[1], (ORB - ORB * s) % 128, 1)
                B2[s, kind] = jnp.where(lane < ORB, even, odd)
                B2[s + 4, kind] = lanes_from(rows, NX * s)

    def reduce_slab():
        copies = []
        for d in range(1, SLABS):
            s = (slab + d) % SLABS
            copies.append(
                send(B2.at[s], R2.at[d - 1], r2_s.at[d - 1], r2_r.at[d - 1], to_slab(s))
            )
        return copies

    def finish(arrived):
        for copy in arrived:
            copy.wait_recv()
        for kind, out in enumerate((corr_ref, proj_ref)):
            block = B2[slab, kind]
            for d in range(SLABS - 1):
                block = block + R2[d, kind]
            out[...] = block[:, :NX] * (1.0 / CELLS)

    G[...] = jnp.zeros(G.shape, jnp.float32)
    stage_s(2)
    stage_s(6)
    stage_f(4)

    pl.semaphore_wait(barrier, len(partners))
    pots = [
        send(pot_ref.at[pl.ds(4, 8)], V_in.at[0], pot_s.at[0], pot_r.at[0], to_slab(up)),
        send(pot_ref.at[pl.ds(0, 8)], V_in.at[1], pot_s.at[1], pot_r.at[1], to_slab(down)),
    ]
    halos = []
    for t in range(2):
        halos.append((
            send(O.at[pl.ds(16 - 2 * t, 2)], O.at[pl.ds(4 - 2 * t, 2)],
                 halo_s.at[0, t], halo_r.at[0, t], to_slab(up)),
            send(O.at[pl.ds(6 + 2 * t, 2)], O.at[pl.ds(18 + 2 * t, 2)],
                 halo_s.at[1, t], halo_r.at[1, t], to_slab(down)),
        ))
    for side in range(2):

        @pl.when(x_pos == ENDS[side])
        def _():
            to_relay(side).start()

        @pl.when(x_pos != ENDS[side])
        def _():
            direct(side).start()

    f0 = swap(0, 0)

    for copy in halos[0]:
        copy.wait_recv()
    stage_s(0, 10)
    stage_f(2, 8)
    f1 = swap(0, 1)
    stage_a(4)
    a0 = swap(1, 0)
    pass_on(0, f0)

    for copy in pots:
        copy.wait_recv()
    for n in range(4):
        fill(n - 4, V_in[0, 4 + n : 5 + n, :])
        fill(12 + n, V_in[1, n : n + 1, :])
    for copy in halos[1]:
        copy.wait_recv()
    stage_s(-2, 12)
    stage_f(0, 10)
    f2 = swap(0, 2)
    store = pltpu.make_async_copy(F.at[pl.ds(2, PLANES)], filt_hbm, out_sem)
    store.start()
    stage_a(2, 8)
    a1 = swap(1, 1)
    pass_on(1, f1)
    pass_halo()

    for side in range(2):
        direct(side).wait_recv()
    stage_s(-4, 14)
    stage_f(-2, 12)
    stage_a(0, 10)
    a2 = swap(1, 2)
    pass_on(3, a0)
    pass_on(2, f2)

    forward(0, 0).wait_recv()
    gram_own(0)
    pass_far(1)

    @pl.when(jnp.logical_not(first))
    def _():
        wait_across(0)
        wait_across(3)
        gram(0, 1, 0, 1, RA_far)
        early().start()

    forward(1, 0).wait_recv()
    swap_wait(a1)
    gram_own(1)
    gram_far(1)
    forward(2, 0).wait_recv()
    gram_own(2, (0,))
    pass_far(2)

    @pl.when(first)
    def _():
        early().wait_recv()
        G[1] = G[1] + G_far[...]

    gram_far(2, (0,))
    reduce_band(0)
    swap_wait(a2)
    gram_own(2, (1,))
    gram_far(2, (1,), False)
    reduce_band(1)
    reduce_rows(0)
    reduce_rows(1)
    finish(reduce_slab())

    for copy in sends:
        copy.wait_send()
    for side in range(2):
        direct(side).wait_send()

        @pl.when(x_pos == RELAYS[side])
        def _():
            from_relay(side).wait_send()

    for q in range(3):
        forward(q, 0).wait_send()

    @pl.when(first)
    def _():
        for q in (1, 2):
            forward(q, 1).wait_send()
        for kind in range(2):
            for d in PEERS:
                to_row(kind, d, 384).wait_send()
            for row in range(4):
                for side in range(2):
                    cross(kind, row, side).wait_send()
        for row in range(4):
            across(0, row, landed(0, row)).wait_send()
            across(3, row, landed(3, row)).wait_send()

    @pl.when(jnp.logical_not(first))
    def _():
        for slot in (1, 2):
            for row in range(4):
                across(slot, row, landed(slot, row)).wait_send()
        early().wait_send()
        for kind in range(2):
            for d in PEERS:
                to_row(kind, d, 256).wait_send()

    store.wait()


def local(orbitals, potential):
    f32 = jnp.float32
    dma = pltpu.SemaphoreType.DMA
    peers = len(PEERS)
    shapes = (
        pltpu.VMEM((PLANES, ORB, NXY), f32),
        pltpu.VMEM((ORB, NX), f32),
        pltpu.VMEM((ORB, NX), f32),
    )
    results = pl.pallas_call(
        kernel,
        out_shape=shapes,
        in_specs=[
            pl.BlockSpec(memory_space=pl.ANY),
            pl.BlockSpec(memory_space=pltpu.VMEM),
            pl.BlockSpec(memory_space=pl.ANY),
        ],
        out_specs=(
            pl.BlockSpec(memory_space=pltpu.VMEM),
            pl.BlockSpec(memory_space=pltpu.VMEM),
            pl.BlockSpec(memory_space=pltpu.VMEM),
        ),
        scratch_shapes=[
            pltpu.VMEM((PLANES + 12, ORB, NXY), f32),
            pltpu.VMEM((2, 2, ORB, NXY), f32),
            pltpu.VMEM((3, 512, 256), jnp.bfloat16),
            pltpu.VMEM((2, 8, NXY), f32),
            pltpu.VMEM((PLANES + 8, 8, NXY), f32),
            pltpu.VMEM((PLANES + 8, ORB, NXY), f32),
            pltpu.VMEM((PLANES + 4, ORB, NXY), f32),
            pltpu.VMEM((PLANES, ORB, NXY), f32),
            pltpu.VMEM((3, 2, 4, 2, ORB, NXY), f32),
            pltpu.VMEM((3, 4, ORB, NXY), f32),
            pltpu.VMEM((4, ORB, NXY), f32),
            pltpu.VMEM((2, 2, ROWS, HALF_ORB), f32),
            pltpu.VMEM((2, ROWS, HALF_ORB), f32),
            pltpu.VMEM((2, ROWS, 2 * HALF_ORB), f32),
            pltpu.VMEM((2, peers, ORB, 2 * HALF_ORB), f32),
            pltpu.VMEM((2, 8, ORB, 128), f32),
            pltpu.VMEM((2, 8, ORB, 128), f32),
            pltpu.VMEM((SLABS, 2, ORB, 128), f32),
            pltpu.VMEM((SLABS - 1, 2, ORB, 128), f32),
            dma, dma, dma,
            dma((2, 3)), dma((2, 3)),
            dma((2,)), dma((2,)),
            dma((2,)), dma((2,)),
            dma((2, 3, peers, 2)), dma((2, 3, peers, 2)),
            dma((2, 3, 2)),
            dma((3, 2)), dma((3, 2)),
            dma((4, 4)), dma((4, 4)),
            dma, dma,
            dma((2, peers)), dma((2, peers)),
            dma((2, 8)), dma((2, 8)),
            dma((SLABS - 1,)), dma((SLABS - 1,)),
        ],
        compiler_params=pltpu.CompilerParams(
            collective_id=0, has_side_effects=True, vmem_limit_bytes=56 << 20
        ),
        cost_estimate=pl.CostEstimate(
            flops=3_500_000_000, bytes_accessed=6_000_000, transcendentals=0
        ),
    )(jnp.transpose(orbitals, (1, 0, 2)), potential, plane_table())
    filtered, correlation, projected = results
    return jnp.transpose(filtered, (1, 0, 2)), correlation, projected


def solution(mesh):
    return jax.shard_map(
        local,
        mesh=mesh,
        in_specs=(P("band", "slab", None), P("slab", None)),
        out_specs=(P("band", "slab", None), P("band", "slab"), P("band", "slab")),
        check_vma=False,
    )
```

```python
import jax
import jax.numpy as jnp
import ml_dtypes
import numpy as np
from jax import lax
from jax.experimental import pallas as pl
from jax.experimental.pallas import tpu as pltpu
from jax.sharding import PartitionSpec as P

NX = 48
NXY = 2304
ORB = 24
PLANES = 12
SLABS = 8
HALF = NXY // 2
CHUNK = 384
CELLS = 221184

SPACING = 0.32
STENCIL = 1.0 / (12.0 * SPACING * SPACING)
CENTER = 38.0
HALF_WIDTH = 42.0
NEAR = -0.5 * STENCIL / HALF_WIDTH
MESH = pl.DeviceIdType.MESH

CHUNK_BASE = (4, 2, 0)
CHUNK_STRIDE = (0, 4, 8)
ENDS = (3, 0)
RELAYS = (1, 2)
PEERS = (1, 3, 2)
HALF_ORB = 192
ROWS = 96


def plane_table():
    table = np.zeros((3, 512, 256), np.float32)
    for r in range(3):
        for n in range(256):
            cell = 256 * r + n
            row, x = cell // NX, cell % NX
            for offset, weight in ((1, 16.0), (2, -1.0), (-1, 16.0), (-2, -1.0)):
                table[r, row * NX + (x + offset) % NX - 256 * r + 128, n] += weight
                table[r, n + 128 + offset * NX, n] += weight
    return table.astype(ml_dtypes.bfloat16)


def dot_nt(a, b):
    return lax.dot_general(a, b, (((1,), (1,)), ((), ())), preferred_element_type=jnp.float32)


def halves(a):
    high = a.astype(jnp.bfloat16)
    return high, (a - high.astype(jnp.float32)).astype(jnp.bfloat16)


def kernel(
    orb_hbm, pot_ref, table_hbm, filt_hbm, corr_ref, proj_ref,
    O, relay, T, V_in, W, S, F, A, RF, RA, RA_far, G, G_far, SB, R1, XB, XR, B2, R2,
    load_sem, table_sem, out_sem, halo_s, halo_r, relay_s, relay_r, pot_s, pot_r, swap_s, swap_r, own_sem, fwd_s, fwd_r,
    far_s, far_r, early_s, early_r, r1_s, r1_r, x_s, x_r, r2_s, r2_r,
):
    band, slab = lax.axis_index("band"), lax.axis_index("slab")
    chip, core = band // 2, band % 2
    z_hi, y = chip // 4, chip % 4

    def to_band(z, row, side):
        return {"band": z * 8 + row * 2 + side, "slab": slab}

    def to_slab(s):
        return {"band": band, "slab": s}

    load = pltpu.make_async_copy(orb_hbm, O.at[pl.ds(6, PLANES)], load_sem)
    load.start()
    table_load = pltpu.make_async_copy(table_hbm, T, table_sem)
    table_load.start()

    up, down = (slab + 1) % SLABS, (slab + SLABS - 1) % SLABS
    partners = [to_band(z_hi, (y + d) % 4, core) for d in PEERS]
    partners.append(to_band(z_hi, y, 1 - core))
    partners += [to_band(1 - z_hi, row, side) for row in range(4) for side in range(2)]
    partners += [to_slab((slab + d) % SLABS) for d in range(1, SLABS)]
    x_pos, z_lo = slab % 4, slab // 4

    def halo_copy(src, dst, s_sem, r_sem, where):
        return pltpu.make_async_remote_copy(
            src_ref=src, dst_ref=dst, send_sem=s_sem, recv_sem=r_sem,
            device_id=to_slab(where), device_id_type=MESH,
        )

    def outer(side):
        return O.at[pl.ds((12, 10)[side], 2)], O.at[pl.ds((0, 22)[side], 2)]

    def direct(side):
        src, dst = outer(side)
        return halo_copy(src, dst, halo_s.at[side, 2], halo_r.at[side, 2], (up, down)[side])

    def to_relay(side):
        return halo_copy(outer(side)[0], relay.at[side], halo_s.at[side, 2], relay_r.at[side],
                         (1 - z_lo) * 4 + RELAYS[side])

    def from_relay(side):
        return halo_copy(relay.at[side], outer(side)[1], relay_s.at[side], halo_r.at[side, 2],
                         z_lo * 4 + ENDS[1 - side])

    def pass_halo():
        for side in range(2):

            @pl.when(x_pos == RELAYS[side])
            def _():
                to_relay(side).wait_recv()
                from_relay(side).start()

    barrier = pltpu.get_barrier_semaphore()
    for partner in partners:
        pl.semaphore_signal(barrier, inc=1, device_id=partner, device_id_type=MESH)

    sends = []

    def send(src, dst, s_sem, r_sem, where):
        copy = pltpu.make_async_remote_copy(
            src_ref=src, dst_ref=dst, send_sem=s_sem, recv_sem=r_sem,
            device_id=where, device_id_type=MESH,
        )
        copy.start()
        sends.append(copy)
        return copy

    def fill(z, row):
        weight = (row + (45.0 * STENCIL - CENTER)) * (1.0 / HALF_WIDTH)
        W[z + 4] = jnp.broadcast_to(weight, (8, NXY))

    for z in range(PLANES):
        fill(z, pot_ref[z : z + 1, :])

    table_load.wait()
    load.wait()

    def stage(src, src_off, starts, emit):
        count = 4 // len(starts)

        def planes(ref, off, rows, lanes):
            parts = [ref[pl.ds(z + off, count), rows, lanes] for z in starts]
            return parts[0] if len(parts) == 1 else jnp.concatenate(parts, axis=0)

        everything = slice(None)

        def body(i, carry):
            for r in range(3):
                base = i * 768 + 256 * r
                lanes = pl.ds(pl.multiple_of(base, 128), 256)
                left = pl.ds(pl.multiple_of((base + NXY - 128) % NXY, 128), 128)
                right = pl.ds(pl.multiple_of((base + 256) % NXY, 128), 128)
                v = planes(src, src_off, everything, lanes)
                wide = jnp.concatenate(
                    [planes(src, src_off, everything, left), v, planes(src, src_off, everything, right)],
                    axis=2,
                ).reshape(4 * ORB, 512)
                flat = jnp.dot(
                    jnp.concatenate(halves(wide), axis=0), T[r], preferred_element_type=jnp.float32
                )
                lap = (flat[: 4 * ORB] + flat[4 * ORB :]).reshape(4, ORB, 256)
                near = planes(src, src_off - 1, everything, lanes) + planes(src, src_off + 1, everything, lanes)
                far = planes(src, src_off - 2, everything, lanes) + planes(src, src_off + 2, everything, lanes)
                weight = planes(W, 4, everything, lanes)
                weight = jnp.concatenate([weight, weight, weight], axis=1)
                emit(lanes, NEAR * (lap + (16.0 * near - far)) + weight * v, v)
            return carry

        lax.fori_loop(0, 3, body, 0)

    def put(ref, off, starts, lanes, value):
        count = 4 // len(starts)
        for n, z in enumerate(starts):
            ref[pl.ds(z + off, count), :, lanes] = value[n * count : (n + 1) * count]

    def stage_s(*starts):
        def emit(lanes, h, v):
            put(S, 4, starts, lanes, h)

        stage(O, 6, starts, emit)

    def stage_f(*starts):
        count = 4 // len(starts)

        def emit(lanes, h, v):
            old = jnp.concatenate([O[pl.ds(z + 6, count), :, lanes] for z in starts], axis=0)
            put(F, 2, starts, lanes, 2.0 * h - old)

        stage(S, 4, starts, emit)

    def stage_a(*starts):
        def emit(lanes, h, v):
            put(A, 0, starts, lanes, HALF_WIDTH * h + CENTER * v)

        stage(F, 2, starts, emit)

    first = z_hi == 0

    def across(slot, row, piece):
        dst = RA_far.at[row] if slot == 3 else RF.at[slot, 1, row, core]
        return pltpu.make_async_remote_copy(
            src_ref=piece, dst_ref=dst,
            send_sem=far_s.at[slot, row], recv_sem=far_r.at[slot, row],
            device_id=to_band(1 - z_hi, y, core), device_id_type=MESH,
        )

    def sends_across(slot):
        return first if slot in (0, 3) else jnp.logical_not(first)

    def takes_across(slot):
        return jnp.logical_not(first) if slot in (0, 3) else first

    def landed(slot, row):
        return RA.at[0, row] if slot == 3 else RF.at[slot, 0, row, core]

    def swap(kind, q):
        src, off = ((F, 2), (A, 0))[kind]

        def part(row, n):
            plane = CHUNK_BASE[q] + row + CHUNK_STRIDE[q] * (row // 2)
            return src.at[plane + off, :, pl.ds(n * HALF, HALF)]

        def place(n):
            lanes = pl.ds(n * HALF, HALF)
            return RF.at[q, 0, y, core, :, lanes] if kind == 0 else RA.at[q, y, :, lanes]

        copies = []
        for n in range(2):
            for d in PEERS:
                row = (y + d) % 4
                copies.append(
                    send(part(row, n), place(n), swap_s.at[kind, q, d - 1, n], swap_r.at[kind, q, d - 1, n],
                         to_band(z_hi, row, core))
                )
        for n in range(2):
            own = pltpu.make_async_copy(part(y, n), place(n), own_sem.at[kind, q, n])
            own.start()
            copies.append(own)
        if kind == 0 or q == 0:
            slot = 3 if kind else q

            @pl.when(sends_across(slot))
            def _():
                plane = CHUNK_BASE[q] + y + CHUNK_STRIDE[q] * (y // 2)
                across(slot, y, src.at[plane + off]).start()

        return copies

    def swap_wait(copies):
        for copy in copies[:-2]:
            copy.wait_recv()
        for own in copies[-2:]:
            own.wait()

    def forward(q, half):
        piece = RF.at[q, half, :, core]
        return pltpu.make_async_remote_copy(
            src_ref=piece, dst_ref=piece, send_sem=fwd_s.at[q, half], recv_sem=fwd_r.at[q, half],
            device_id=to_band(z_hi, y, 1 - core), device_id_type=MESH,
        )

    def pass_on(slot, copies):
        for n, d in enumerate(PEERS):
            copies[n].wait_recv()
            copies[n + 3].wait_recv()

            @pl.when(sends_across(slot))
            def _():
                row = (y + 4 - d) % 4
                across(slot, row, landed(slot, row)).start()

        for own in copies[-2:]:
            own.wait()
        if slot < 3:
            forward(slot, 0).start()

    def wait_across(slot):
        for row in range(4):
            across(slot, row, landed(slot, row)).wait_recv()

    def pass_far(q):
        @pl.when(first)
        def _():
            wait_across(q)
            forward(q, 1).start()

    def gram(q, half, columns, f_rows, a_rows, kinds=(0, 1)):
        count = len(kinds) * ROWS

        def body(k, carry):
            lanes = pl.ds(pl.multiple_of(k * 1152, 128), 1152)
            f_high, f_low = halves(RF[q, columns, :, :, :, lanes].reshape(HALF_ORB, 1152))
            rows = [RF[q, f_rows, :, core, :, lanes] if kind == 0 else a_rows[:, :, lanes] for kind in kinds]
            rows = rows[0] if len(kinds) == 1 else jnp.concatenate(rows, axis=0)
            high, low = halves(rows.reshape(count, 1152))
            both = dot_nt(jnp.concatenate([high, low], axis=0), f_high)
            part = (both[:count] + both[count:]) + dot_nt(high, f_low)
            for n, kind in enumerate(kinds):
                G[half, kind] = G[half, kind] + part[n * ROWS : (n + 1) * ROWS]
            return carry

        lax.fori_loop(0, NXY // 1152, body, 0)

    def gram_own(q, kinds=(0, 1)):
        gram(q, 0, 0, 0, RA.at[q], kinds)

    def gram_far(q, kinds=(0, 1), wait=True):
        @pl.when(first)
        def _():
            if wait:
                forward(q, 1).wait_recv()
            gram(q, 1, 1, 0, RA.at[q], kinds)

    def early():
        return pltpu.make_async_remote_copy(
            src_ref=G.at[1], dst_ref=G_far, send_sem=early_s, recv_sem=early_r,
            device_id=to_band(1 - z_hi, y, core), device_id_type=MESH,
        )

    def to_row(kind, d, width):
        row = (y + d) % 4
        return pltpu.make_async_remote_copy(
            src_ref=SB.at[kind, pl.ds(pl.multiple_of(row * ORB, 8), ORB), pl.ds(0, width)],
            dst_ref=R1.at[kind, d - 1, :, pl.ds(0, width)],
            send_sem=r1_s.at[kind, d - 1], recv_sem=r1_r.at[kind, d - 1],
            device_id=to_band(z_hi, row, core), device_id_type=MESH,
        )

    def cross(kind, row, side):
        index = row * 2 + side
        return pltpu.make_async_remote_copy(
            src_ref=XB.at[kind, index], dst_ref=XR.at[kind, y * 2 + core],
            send_sem=x_s.at[kind, index], recv_sem=x_r.at[kind, y * 2 + core],
            device_id=to_band(1 - z_hi, row, side), device_id_type=MESH,
        )

    def cross_from(kind, index):
        return pltpu.make_async_remote_copy(
            src_ref=XB.at[kind, index], dst_ref=XR.at[kind, index],
            send_sem=x_s.at[kind, index], recv_sem=x_r.at[kind, index],
            device_id=to_band(1 - z_hi, index // 2, index % 2), device_id_type=MESH,
        )

    def reduce_band(kind):
        SB[kind] = jnp.concatenate([G[0, kind], G[1, kind]], axis=1)

        @pl.when(first)
        def _():
            for d in PEERS:
                to_row(kind, d, 384).start()
            block = jnp.concatenate([G[1, kind], jnp.zeros((128 - ROWS, HALF_ORB), jnp.float32)], axis=0)
            XB[kind] = jnp.transpose(block).reshape(8, ORB, 128)
            for row in range(4):
                for side in range(2):
                    cross(kind, row, side).start()

        @pl.when(jnp.logical_not(first))
        def _():
            for d in PEERS:
                to_row(kind, d, 256).start()

    lane = lax.broadcasted_iota(jnp.int32, (ORB, 128), 1)

    def lanes_from(value, start):
        return pltpu.roll(value, (-start) % value.shape[1], 1)[:, :128]

    def reduce_rows(kind):
        mine = pl.ds(pl.multiple_of(y * ORB, 8), ORB)

        @pl.when(first)
        def _():
            rows = SB[kind, mine]
            for d in PEERS:
                to_row(kind, d, 384).wait_recv()
                rows = rows + R1[kind, d - 1]
            for s in range(SLABS):
                B2[s, kind] = lanes_from(rows, NX * s)

        @pl.when(jnp.logical_not(first))
        def _():
            rows = SB[kind, mine, pl.ds(0, 256)]
            for d in PEERS:
                to_row(kind, d, 256).wait_recv()
                rows = rows + R1[kind, d - 1, :, pl.ds(0, 256)]
            for index in range(8):
                cross_from(kind, index).wait_recv()
            sides = []
            for side in range(2):
                total = XR[kind, side]
                for row in range(1, 4):
                    total = total + XR[kind, 2 * row + side]
                sides.append(total)
            for s in range(4):
                even = lanes_from(sides[0], ORB * s)
                odd = pltpu.roll(sides[1], (ORB - ORB * s) % 128, 1)
                B2[s, kind] = jnp.where(lane < ORB, even, odd)
                B2[s + 4, kind] = lanes_from(rows, NX * s)

    def reduce_slab():
        copies = []
        for d in range(1, SLABS):
            s = (slab + d) % SLABS
            copies.append(
                send(B2.at[s], R2.at[d - 1], r2_s.at[d - 1], r2_r.at[d - 1], to_slab(s))
            )
        return copies

    def finish(arrived):
        for copy in arrived:
            copy.wait_recv()
        for kind, out in enumerate((corr_ref, proj_ref)):
            block = B2[slab, kind]
            for d in range(SLABS - 1):
                block = block + R2[d, kind]
            out[...] = block[:, :NX] * (1.0 / CELLS)

    G[...] = jnp.zeros(G.shape, jnp.float32)
    stage_s(2)
    stage_s(6)
    stage_f(4)

    pl.semaphore_wait(barrier, len(partners))
    pots = [
        send(pot_ref.at[pl.ds(4, 8)], V_in.at[0], pot_s.at[0], pot_r.at[0], to_slab(up)),
        send(pot_ref.at[pl.ds(0, 8)], V_in.at[1], pot_s.at[1], pot_r.at[1], to_slab(down)),
    ]
    halos = []
    for t in range(2):
        halos.append((
            send(O.at[pl.ds(16 - 2 * t, 2)], O.at[pl.ds(4 - 2 * t, 2)],
                 halo_s.at[0, t], halo_r.at[0, t], to_slab(up)),
            send(O.at[pl.ds(6 + 2 * t, 2)], O.at[pl.ds(18 + 2 * t, 2)],
                 halo_s.at[1, t], halo_r.at[1, t], to_slab(down)),
        ))
    for side in range(2):

        @pl.when(x_pos == ENDS[side])
        def _():
            to_relay(side).start()

        @pl.when(x_pos != ENDS[side])
        def _():
            direct(side).start()

    f0 = swap(0, 0)

    for copy in halos[0]:
        copy.wait_recv()
    stage_s(0, 10)
    stage_f(2, 8)
    f1 = swap(0, 1)
    stage_a(4)
    a0 = swap(1, 0)
    pass_on(0, f0)

    for copy in pots:
        copy.wait_recv()
    for n in range(4):
        fill(n - 4, V_in[0, 4 + n : 5 + n, :])
        fill(12 + n, V_in[1, n : n + 1, :])
    for copy in halos[1]:
        copy.wait_recv()
    stage_s(-2, 12)
    stage_f(0, 10)
    f2 = swap(0, 2)
    store = pltpu.make_async_copy(F.at[pl.ds(2, PLANES)], filt_hbm, out_sem)
    store.start()
    stage_a(2, 8)
    a1 = swap(1, 1)
    pass_on(1, f1)
    pass_halo()

    for side in range(2):
        direct(side).wait_recv()
    stage_s(-4, 14)
    stage_f(-2, 12)
    stage_a(0, 10)
    a2 = swap(1, 2)
    pass_on(2, f2)
    pass_on(3, a0)

    forward(0, 0).wait_recv()
    gram_own(0)
    pass_far(1)

    @pl.when(jnp.logical_not(first))
    def _():
        wait_across(0)
        wait_across(3)
        gram(0, 1, 0, 1, RA_far)
        early().start()

    forward(1, 0).wait_recv()
    swap_wait(a1)
    gram_own(1)
    gram_far(1)
    forward(2, 0).wait_recv()
    gram_own(2, (0,))
    pass_far(2)

    @pl.when(first)
    def _():
        early().wait_recv()
        G[1] = G[1] + G_far[...]

    gram_far(2, (0,))
    reduce_band(0)
    swap_wait(a2)
    gram_own(2, (1,))
    gram_far(2, (1,), False)
    reduce_band(1)
    reduce_rows(0)
    reduce_rows(1)
    finish(reduce_slab())

    for copy in sends:
        copy.wait_send()
    for side in range(2):
        direct(side).wait_send()

        @pl.when(x_pos == RELAYS[side])
        def _():
            from_relay(side).wait_send()

    for q in range(3):
        forward(q, 0).wait_send()

    @pl.when(first)
    def _():
        for q in (1, 2):
            forward(q, 1).wait_send()
        for kind in range(2):
            for d in PEERS:
                to_row(kind, d, 384).wait_send()
            for row in range(4):
                for side in range(2):
                    cross(kind, row, side).wait_send()
        for row in range(4):
            across(0, row, landed(0, row)).wait_send()
            across(3, row, landed(3, row)).wait_send()

    @pl.when(jnp.logical_not(first))
    def _():
        for slot in (1, 2):
            for row in range(4):
                across(slot, row, landed(slot, row)).wait_send()
        early().wait_send()
        for kind in range(2):
            for d in PEERS:
                to_row(kind, d, 256).wait_send()

    store.wait()


def local(orbitals, potential):
    f32 = jnp.float32
    dma = pltpu.SemaphoreType.DMA
    peers = len(PEERS)
    shapes = (
        pltpu.VMEM((PLANES, ORB, NXY), f32),
        pltpu.VMEM((ORB, NX), f32),
        pltpu.VMEM((ORB, NX), f32),
    )
    results = pl.pallas_call(
        kernel,
        out_shape=shapes,
        in_specs=[
            pl.BlockSpec(memory_space=pl.ANY),
            pl.BlockSpec(memory_space=pltpu.VMEM),
            pl.BlockSpec(memory_space=pl.ANY),
        ],
        out_specs=(
            pl.BlockSpec(memory_space=pltpu.VMEM),
            pl.BlockSpec(memory_space=pltpu.VMEM),
            pl.BlockSpec(memory_space=pltpu.VMEM),
        ),
        scratch_shapes=[
            pltpu.VMEM((PLANES + 12, ORB, NXY), f32),
            pltpu.VMEM((2, 2, ORB, NXY), f32),
            pltpu.VMEM((3, 512, 256), jnp.bfloat16),
            pltpu.VMEM((2, 8, NXY), f32),
            pltpu.VMEM((PLANES + 8, 8, NXY), f32),
            pltpu.VMEM((PLANES + 8, ORB, NXY), f32),
            pltpu.VMEM((PLANES + 4, ORB, NXY), f32),
            pltpu.VMEM((PLANES, ORB, NXY), f32),
            pltpu.VMEM((3, 2, 4, 2, ORB, NXY), f32),
            pltpu.VMEM((3, 4, ORB, NXY), f32),
            pltpu.VMEM((4, ORB, NXY), f32),
            pltpu.VMEM((2, 2, ROWS, HALF_ORB), f32),
            pltpu.VMEM((2, ROWS, HALF_ORB), f32),
            pltpu.VMEM((2, ROWS, 2 * HALF_ORB), f32),
            pltpu.VMEM((2, peers, ORB, 2 * HALF_ORB), f32),
            pltpu.VMEM((2, 8, ORB, 128), f32),
            pltpu.VMEM((2, 8, ORB, 128), f32),
            pltpu.VMEM((SLABS, 2, ORB, 128), f32),
            pltpu.VMEM((SLABS - 1, 2, ORB, 128), f32),
            dma, dma, dma,
            dma((2, 3)), dma((2, 3)),
            dma((2,)), dma((2,)),
            dma((2,)), dma((2,)),
            dma((2, 3, peers, 2)), dma((2, 3, peers, 2)),
            dma((2, 3, 2)),
            dma((3, 2)), dma((3, 2)),
            dma((4, 4)), dma((4, 4)),
            dma, dma,
            dma((2, peers)), dma((2, peers)),
            dma((2, 8)), dma((2, 8)),
            dma((SLABS - 1,)), dma((SLABS - 1,)),
        ],
        compiler_params=pltpu.CompilerParams(
            collective_id=0, has_side_effects=True, vmem_limit_bytes=56 << 20
        ),
        cost_estimate=pl.CostEstimate(
            flops=3_500_000_000, bytes_accessed=6_000_000, transcendentals=0
        ),
    )(jnp.transpose(orbitals, (1, 0, 2)), potential, plane_table())
    filtered, correlation, projected = results
    return jnp.transpose(filtered, (1, 0, 2)), correlation, projected


def solution(mesh):
    return jax.shard_map(
        local,
        mesh=mesh,
        in_specs=(P("band", "slab", None), P("slab", None)),
        out_specs=(P("band", "slab", None), P("band", "slab"), P("band", "slab")),
        check_vma=False,
    )
```
